32 devices in a mesh: dp: 16 (over z, y, core), group: 2 (over x).
Axes of the slice: x: 2, y: 2, z: 4, core: 2. Of those that a mesh axis runs over, the one named last changes fastest.
Arguments:
- inputs_t: bfloat16 [64, 128, 2048], P(None, 'group', 'dp'), may hold values from -6 to 6
- grad_proj: bfloat16 [2, 112, 128, 2048], P(None, None, None, 'dp'), may hold values from -6 to 6
- stored_blocks: bfloat16 [16, 2, 128, 128], P('dp', None, 'group'), may hold values from -0.25 to 0.25
- block_scales: float32 [16, 2], P('dp'), may hold values from 0.5 to 2
- kept_blocks: int32 [2, 3584], replicated, may hold values from 0 to 7167, as said below
- assignment: int32 [24], replicated, may hold values from 0 to 7167, as said below
- owner_counts: int32 [16], replicated, may hold values from 1 to 2, 24 in all
Outputs:
- grad_inputs_t: bfloat16 [64, 128, 2048], P(None, 'group', 'dp')
- block_grads: float32 [16, 2, 128, 128], P('dp', None, 'group')
- scale_grads: float32 [16, 2], P('dp')
The draws below stay inside these ranges and needn't reach their ends.
Inputs may be any that keep to these rules, and one draw needn't show every extreme that they name: `kept_blocks`: row m lists, in ascending order, 3584 distinct kept blocks of projection m (0 gate, 1 up); block b covers features from 128 * (b // 112) and hidden units from 128 * (b % 112). `assignment`: 24 distinct entries; entry e stands for block kept_blocks[e // 3584, e % 3584]; owner o holds in its slots 0 to owner_counts[o] - 1 the entries at positions offset(o) onward, offset(o) being the sum of the counts of the owners before o. `owner_counts`: the counts sum to 24.
All inputs are finite; a program needn't handle non-finite values.
Results may differ from the reference program's by a relative error of at most 0.0049.
Values may be sent and summed in bfloat16 or wider, within the bound.
No kernel may reach another device: no remote copies, remote signals or barrier semaphores. Data moves between devices by JAX's collectives and lax.ppermute only.
A program may use at most 64 MiB of HBM per device.

```python
import math
import jax
import jax.numpy as jnp
import numpy as np
from jax import lax

BLK = 128
HB = 112
CAP = 2
RB = 64
KEEP = 3584
OWNERS = 16
NB = 24
TOKENS = 2048


def draw_kept_blocks(key, part):
    key = jax.random.fold_in(key, 11)
    total = RB * HB
    chosen_rows = []
    for which in range(2):
        middle = jax.random.permutation(jax.random.fold_in(key, which), total - 2).astype(jnp.int32) + 2
        ranks = jnp.concatenate([jnp.zeros((1,), jnp.int32), middle, jnp.ones((1,), jnp.int32)])
        chosen = jnp.nonzero(ranks < KEEP, size=KEEP)[0]
        chosen_rows.append(chosen.astype(jnp.int32))
    return jnp.stack(chosen_rows)


def draw_assignment(key, part):
    key = jax.random.fold_in(key, 13)
    inner = jax.random.permutation(jax.random.fold_in(key, 1), 2 * KEEP - 2).astype(jnp.int32) + 1
    ends = jnp.array([0, 2 * KEEP - 1], jnp.int32)
    entries = jnp.concatenate([ends, inner[:NB - 2]])
    order = jax.random.permutation(jax.random.fold_in(key, 2), NB)
    return entries[order].astype(jnp.int32)


def level_of(rng, dims, pieces, least, largest):
    def one(axis_at, parts):
        draws = jax.random.uniform(jax.random.fold_in(jax.random.fold_in(rng, 6), axis_at), (parts,), jnp.float32, least / len(pieces), largest / len(pieces))
        return jnp.repeat(jnp.exp(draws), dims[axis_at] // parts).reshape((-1,) + (1,) * (len(dims) - axis_at - 1))

    loudness = one(*pieces[0])
    for cut in pieces[1:]:
        loudness = loudness * one(*cut)
    return loudness


def length_profile(count, total, limit, lean):
    portions = [(1 << 20) // math.isqrt(grade ** lean) + 1 for grade in range(2, count + 1)]
    rest, counts = total - limit - (count - 1), [1] * (count - 1)
    while rest > 0:
        movable = [i for i in range(count - 1) if counts[i] < limit]
        whole, budget = sum([portions[i] for i in movable]), rest
        for i in movable:
            addition = min(limit - counts[i], max(1, budget * portions[i] // whole), rest)
            counts[i] = counts[i] + addition
            rest = rest - addition
    return np.array([limit] + counts)


def uneven_parts(own_key, amount, total, most, skew):
    if amount == 2:
        one = jax.random.randint(own_key, (), max(1, total - most), min(most, total - 1) + 1)
        return jnp.stack([one, total - one])
    tallies = jnp.asarray(length_profile(amount, total, most, skew), jnp.int32)
    couples = (amount - 1) // 2
    source_of, taker = tallies[1:1 + 2 * couples:2], tallies[2:2 + 2 * couples:2]
    margin = jnp.minimum(source_of - 1, most - taker)
    passed = jax.random.randint(jax.random.fold_in(own_key, 1), (couples,), 0, 1 << 20) % (margin + 1)
    tallies = tallies.at[1:1 + 2 * couples:2].set(source_of - passed).at[2:2 + 2 * couples:2].set(taker + passed)
    return tallies[jax.random.permutation(jax.random.fold_in(own_key, 2), amount)]


def normal_values(own_key, shape, deviation, limit, cuts=(), held_as=jnp.bfloat16):
    values = deviation * jax.random.normal(own_key, shape, jnp.float32)
    if cuts:
        values = values * level_of(own_key, shape, cuts, -0.22, 0.18)
    return jnp.clip(values, -limit, limit).astype(held_as)


def setup_inputs(seed: int = 0) -> dict:
    streams_of = jax.random.split(jax.random.key(seed), 8)
    inputs_t = normal_values(streams_of[0], (RB, BLK, TOKENS), 1.0, 6.0, ((1, 2), (2, 16)))
    grad_proj = normal_values(streams_of[1], (2, HB, BLK, TOKENS), 1.0, 6.0, ((3, 16),))
    stored_blocks = normal_values(streams_of[2], (OWNERS, CAP, BLK, BLK), (4 * BLK) ** -0.5, 0.25, ((0, 16), (2, 2)))
    block_scales = jnp.clip(jnp.exp(math.log(2.0) - 1.3862944 * jax.random.uniform(streams_of[3], (OWNERS, CAP), jnp.float32) ** level_of(streams_of[3], (OWNERS, CAP), ((0, 16),), -0.2, 0.2)), 0.5, 2.0)
    kept_blocks = draw_kept_blocks(jax.random.fold_in(streams_of[7], 71), 0)
    assignment = draw_assignment(jax.random.fold_in(streams_of[7], 71), 0)
    owner_counts = uneven_parts(streams_of[6], OWNERS, NB, CAP, 1).astype(jnp.int32)
    return dict(inputs_t=inputs_t, grad_proj=grad_proj, stored_blocks=stored_blocks, block_scales=block_scales, kept_blocks=kept_blocks, assignment=assignment, owner_counts=owner_counts)


def slot_tables(kept_blocks, assignment, owner_counts, slot_count):
    offsets = jnp.cumsum(owner_counts) - owner_counts
    slot_column = jnp.arange(slot_count, dtype=jnp.int32)
    live_slot = slot_column[None, :] < owner_counts[:, None]
    position = jnp.clip(offsets[:, None] + slot_column[None, :], 0, assignment.shape[0] - 1).astype(jnp.int32)
    entry_id = assignment[position]
    matrix = entry_id // KEEP
    kept_index = kept_blocks[matrix, entry_id % KEEP]
    return (live_slot, matrix, kept_index // HB, kept_index % HB)

def reference(inputs_t, grad_proj, stored_blocks, block_scales, kept_blocks, assignment, owner_counts):
    live_slot, matrix, row_block, col_block = slot_tables(kept_blocks, assignment, owner_counts, CAP)
    scaled = (block_scales[:, :, None, None] * stored_blocks.astype(jnp.float32)).astype(jnp.bfloat16)
    zero_index = jnp.zeros((), jnp.int32)

    def slot_step(totals, slot_data):
        block_now, live_now, matrix_now, row_now, column_now = slot_data
        columns = lax.dynamic_slice(grad_proj, (matrix_now.astype(jnp.int32), column_now.astype(jnp.int32), zero_index, zero_index), (1, 1, BLK, TOKENS))[0, 0]
        contrib = jnp.dot(block_now, columns, preferred_element_type=jnp.float32)
        contrib = jnp.where(live_now, contrib, 0.0)
        row_index = row_now.astype(jnp.int32)
        current = lax.dynamic_index_in_dim(totals, row_index, 0, keepdims=False)
        totals = lax.dynamic_update_index_in_dim(totals, current + contrib, row_index, 0)
        input_rows = lax.dynamic_index_in_dim(inputs_t, row_index, 0, keepdims=False)
        slot_grad = lax.dot_general(input_rows, columns, (((1,), (1,)), ((), ())), preferred_element_type=jnp.float32)
        return (totals, slot_grad)
    totals, slot_grads = lax.scan(slot_step, jnp.zeros((RB, BLK, TOKENS), jnp.float32), (scaled.reshape(-1, BLK, BLK), live_slot.reshape(-1), matrix.reshape(-1), row_block.reshape(-1), col_block.reshape(-1)))
    grad_inputs_t = totals.astype(jnp.bfloat16)
    gradient = (slot_grads * (1.0 / math.sqrt(TOKENS))).reshape(OWNERS, CAP, BLK, BLK)
    block_grads = jnp.where(live_slot[:, :, None, None], block_scales[:, :, None, None] * gradient, 0.0)
    scale_grads = jnp.where(live_slot, lax.optimization_barrier(jnp.sum(stored_blocks.astype(jnp.float32) * gradient, axis=(2, 3))), 0.0)
    return (grad_inputs_t, block_grads, scale_grads)
```

```python
import functools
import math

import jax
import jax.numpy as jnp
from jax import lax
from jax.experimental import pallas as pl
from jax.experimental.pallas import tpu as pltpu
from jax.sharding import PartitionSpec as P

VMEM_LIMIT = 48 * 1024 * 1024
TAIL = 16
UNIT = 2.0**15
SMEM_SPEC = pl.BlockSpec(memory_space=pltpu.SMEM)
VMEM_SPEC = pl.BlockSpec(memory_space=pltpu.VMEM)
ANY_SPEC = pl.BlockSpec(memory_space=pl.ANY)
HBM_SPEC = pl.BlockSpec(memory_space=pltpu.HBM)


def magic_divide(value, divisor, limit):
    shift = 20
    factor = -(-(1 << shift) // divisor)
    assert limit * factor < 1 << 31
    assert all((v * factor) >> shift == v // divisor for v in range(limit))
    return (value * factor) >> shift


def partial_kernel(
    kept_hbm, assign_hbm, counts_hbm, x_hbm, grad_ref, stored_hbm, scales_hbm,
    near_keep, near_send, far_keep, far_send, cols_ref, tab_ref, scaled_ref, stored_ref, scale_rows,
    part_ref, x_ref, scales_ref, kept, assign, counts, slot_ref, sem, index_sems, x_sem
):
    x_copy = pltpu.make_async_copy(x_hbm, x_ref, x_sem)
    index_copies = [
        pltpu.make_async_copy(source, target, index_sems.at[i])
        for i, (source, target) in enumerate(
            (
                (assign_hbm, assign),
                (kept_hbm, kept),
                (counts_hbm, counts),
                (scales_hbm, scales_ref),
                (stored_hbm, stored_ref),
            )
        )
    ]
    for copy in index_copies:
        copy.start()
    x_copy.start()
    keep_count = kept.shape[1]
    hid_blocks = grad_ref.shape[1]
    total = x_ref.shape[0] * hid_blocks
    owners = counts.shape[0]
    entries = assign.shape[0]
    outer, cap = near_keep.shape[:2]
    me = lax.axis_index("dp")
    part_ref[...] = jnp.zeros_like(part_ref)
    for copy in index_copies[:2]:
        copy.wait()

    def fetch_step(p, carry):
        entry = assign[p]
        matrix = jnp.where(entry >= keep_count, 1, 0)
        block = kept[matrix, entry - matrix * keep_count]
        row = magic_divide(block, hid_blocks, total)
        column = block - row * hid_blocks
        pltpu.make_async_copy(grad_ref.at[matrix, column], cols_ref.at[p], sem).start()
        tab_ref[0, p] = row
        return carry

    lax.fori_loop(0, entries, fetch_step, 0, unroll=min(entries, 24))
    for copy in index_copies[2:]:
        copy.wait()

    def owner_step(owner, offset):
        kind = (owner & 3) ^ (me & 3)
        if is_paired(outer):
            step_to = step_from = (owner >> 2) ^ (me >> 2)
        else:
            away = (owner >> 2) - (me >> 2)
            step_to = jnp.where(away < 0, away + outer, away)
            step_from = jnp.where(away > 0, outer - away, -away)
        for c in range(cap):

            @pl.when(c < counts[owner])
            def _():
                p = offset + c
                slot_ref[p] = (kind * outer + step_to) * cap + c
                tab_ref[1, p] = kind
                tab_ref[2, p] = step_from
                tab_ref[3, p] = c

        return offset + counts[owner]

    lax.fori_loop(0, owners, owner_step, 0, unroll=min(owners, 16))
    for c in range(cap):
        scaled = scales_ref[0, c] * stored_ref[0, c].astype(jnp.float32)
        scaled_ref[c] = scaled.astype(jnp.bfloat16)
        scale_rows[c] = jnp.full(scale_rows.shape[1:], scales_ref[0, c], jnp.float32)
    x_copy.wait()
    pltpu.make_async_copy(cols_ref, cols_ref, sem).wait()

    def entry_step(p, carry):
        part_ref[slot_ref[p]] = lax.dot_general(
            x_ref[tab_ref[0, p]],
            cols_ref[p],
            (((1,), (1,)), ((), ())),
            preferred_element_type=jnp.float32,
        )
        return carry

    lax.fori_loop(0, entries, entry_step, 0, unroll=min(entries, 24))
    size = outer * cap
    for kind, ref in enumerate((near_keep, near_send, far_keep, far_send)):
        ref[...] = part_ref[kind * size : (kind + 1) * size].reshape(ref.shape)


def encode(total):
    largest = jnp.max(jnp.abs(total), axis=0, keepdims=True)
    power = jnp.ceil(jnp.log2(jnp.maximum(largest, 2.0**-126)))
    power = jnp.clip(power, -126.0, 126.0)
    level = jnp.floor(total * jnp.exp2(-power) * UNIT + 0.5)
    level = jnp.clip(level, -UNIT, UNIT - 1.0)
    return level.astype(jnp.int32).astype(jnp.int16), power


def message_rows(blocks, slab_rows):
    return blocks * slab_rows + -(-blocks // TAIL) * TAIL


def write_message(totals, out_ref):
    blocks, (slab_rows, side) = len(totals), totals[0].shape
    tail_rows = out_ref.shape[0] - blocks * slab_rows
    tail_row = lax.broadcasted_iota(jnp.int32, (tail_rows, side), 0)
    tail = jnp.zeros((tail_rows, side), jnp.float32)
    for i, total in enumerate(totals):
        level, power = encode(total)
        out_ref[i * slab_rows : (i + 1) * slab_rows] = level
        tail = jnp.where(tail_row == i, power, tail)
    out_ref[blocks * slab_rows :] = tail.astype(jnp.int32).astype(jnp.int16)


def read_message(blocks, slab_rows, ref):
    powers = ref[blocks * slab_rows :].astype(jnp.int32).astype(jnp.float32)
    units = jnp.exp2(powers) * (1.0 / UNIT)
    totals = []
    for i in range(blocks):
        level = ref[i * slab_rows : (i + 1) * slab_rows].astype(jnp.int32)
        totals.append(level.astype(jnp.float32) * units[i : i + 1])
    return totals


def far_sum_kernel(keep_ref, got_ref, near_send, out_ref, near_out):
    near_out[...] = near_send[...]
    outer, cap = keep_ref.shape[:2]
    totals = [keep_ref[k, c] + got_ref[k, c] for k in range(outer) for c in range(cap)]
    write_message(totals, out_ref)


def near_sum_kernel(keep_ref, got_ref, far_ref, *out_refs):
    outer, cap, slab_rows, side = keep_ref.shape
    far = read_message(outer * cap, slab_rows, far_ref)
    for step in range(outer):
        totals = [
            keep_ref[step, c] + got_ref[step, c] + far[step * cap + c] for c in range(cap)
        ]
        if step == 0:
            for c in range(cap):
                out_refs[0][c] = totals[c]
        else:
            write_message(totals, out_refs[step])


def add_kernel(own_ref, *refs):
    *got_refs, out_ref = refs
    cap, slab_rows, side = own_ref.shape
    totals = [own_ref[c] for c in range(cap)]
    for got_ref in got_refs:
        totals = [a + b for a, b in zip(totals, read_message(cap, slab_rows, got_ref))]
    for c in range(cap):
        out_ref[c] = totals[c]


def stack_kernel(*refs):
    *in_refs, _, out_ref = refs
    at = 0
    for in_ref in in_refs:
        if in_ref.ndim < out_ref.ndim:
            out_ref[at] = in_ref[...]
            at += 1
        else:
            out_ref[at : at + in_ref.shape[0]] = in_ref[...]
            at += in_ref.shape[0]


def input_grad_kernel(tab_ref, cols_ref, mine, other, block_ref, out_ref, block_out, acc_ref):
    entries = cols_ref.shape[0]
    block_out[...] = block_ref[...]
    acc_ref[...] = jnp.zeros_like(acc_ref)

    def entry_step(p, carry):
        kind, behind, c = tab_ref[1, p], tab_ref[2, p], tab_ref[3, p]
        block = jnp.where(
            (kind & 1) == 0, mine[behind, kind >> 1, c], other[behind, kind >> 1, c]
        )
        row = tab_ref[0, p]
        acc_ref[row] += jnp.dot(block, cols_ref[p], preferred_element_type=jnp.float32)
        return carry

    lax.fori_loop(0, entries, entry_step, 0, unroll=min(entries, 24))
    out_ref[...] = acc_ref[...].astype(out_ref.dtype)


def owner_sum_kernel(norm, scales_ref, stored_ref, own_ref, *refs):
    got_refs, (block_ref, dots_ref) = refs[:-2], refs[-2:]
    cap, slab_rows, side = stored_ref.shape[1:]
    totals = [own_ref[c] for c in range(cap)]
    for got_ref in got_refs:
        totals = [a + b for a, b in zip(totals, read_message(cap, slab_rows, got_ref))]
    for c in range(cap):
        gradient = totals[c] * norm
        block_ref[0, c] = scales_ref[c, 0:1] * gradient
        dots_ref[c : c + 1, :] = jnp.sum(
            stored_ref[0, c].astype(jnp.float32) * gradient, axis=0, keepdims=True
        )


def finish_kernel(dots_ref, got_ref, grads_ref, scale_out):
    del grads_ref
    total = jnp.sum(dots_ref[...] + got_ref[...], axis=1, keepdims=True)
    cap = total.shape[0]
    row = lax.broadcasted_iota(jnp.int32, (cap, cap), 0)
    column = lax.broadcasted_iota(jnp.int32, (cap, cap), 1)
    scale_out[...] = jnp.sum(jnp.where(row == column, total, 0.0), axis=0, keepdims=True)


def cost(microseconds):
    return pl.CostEstimate(
        flops=int(microseconds * 1_153_000_000), bytes_accessed=int(microseconds * 3_690_000), transcendentals=0
    )


def in_hbm(value):
    return pltpu.with_memory_space_constraint(value, pltpu.HBM)


def flipped(value, bit):
    return lax.ppermute(value, "dp", [(i, i ^ bit) for i in range(lax.axis_size("dp"))])


def is_paired(size):
    return size & (size - 1) == 0


def ahead(places, start, step):
    return start ^ step if is_paired(places) else (start + step) % places


def stepped(value, step):
    size = lax.axis_size("dp")
    return lax.ppermute(
        value, "dp", [(i, ahead(size // 4, i // 4, step) * 4 + i % 4) for i in range(size)]
    )


def stacked(name, estimate, after, *values):
    single = min(value.ndim for value in values)
    count = sum(1 if value.ndim == single else value.shape[0] for value in values)
    shape = (count,) + values[0].shape
    return pl.pallas_call(
        stack_kernel,
        out_shape=jax.ShapeDtypeStruct(shape, values[0].dtype),
        in_specs=[VMEM_SPEC] * len(values) + [ANY_SPEC],
        out_specs=VMEM_SPEC,
        compiler_params=pltpu.CompilerParams(vmem_limit_bytes=VMEM_LIMIT),
        cost_estimate=cost(estimate),
        name=name,
    )(*values, after)


def on_device(
    inputs_t, grad_proj, stored_blocks, block_scales, kept_blocks, assignment, owner_counts
):
    row_blocks, slab_rows, tokens_here = inputs_t.shape
    cap, side = stored_blocks.shape[1], stored_blocks.shape[3]
    entries = assignment.shape[0]
    devices = lax.axis_size("dp")
    outer = devices // 4
    norm = 1.0 / math.sqrt(tokens_here * devices)
    params = pltpu.CompilerParams(vmem_limit_bytes=VMEM_LIMIT)
    block_shape = (cap, slab_rows, side)
    side_shape = (outer, cap, slab_rows, side)
    message_shape = (message_rows(cap, slab_rows), side)

    near_keep, near_send, far_keep, far_send, columns, table, scaled, stored, scale_rows = pl.pallas_call(
        partial_kernel,
        out_shape=[jax.ShapeDtypeStruct(side_shape, jnp.float32)] * 4
        + [
            jax.ShapeDtypeStruct((entries, side, tokens_here), jnp.bfloat16),
            jax.ShapeDtypeStruct((4, entries), jnp.int32),
            jax.ShapeDtypeStruct(block_shape, jnp.bfloat16),
            jax.ShapeDtypeStruct(stored_blocks.shape, jnp.bfloat16),
            jax.ShapeDtypeStruct((cap, 8, side), jnp.float32),
        ],
        in_specs=[HBM_SPEC] * 7,
        out_specs=[VMEM_SPEC] * 5 + [SMEM_SPEC] + [VMEM_SPEC] * 3,
        scratch_shapes=[
            pltpu.VMEM((4 * outer * cap, slab_rows, side), jnp.float32),
            pltpu.VMEM(inputs_t.shape, inputs_t.dtype),
            pltpu.SMEM(block_scales.shape, jnp.float32),
            pltpu.SMEM(kept_blocks.shape, jnp.int32),
            pltpu.SMEM(assignment.shape, jnp.int32),
            pltpu.SMEM(owner_counts.shape, jnp.int32),
            pltpu.SMEM((entries,), jnp.int32),
            pltpu.SemaphoreType.DMA,
            pltpu.SemaphoreType.DMA((5,)),
            pltpu.SemaphoreType.DMA,
        ],
        compiler_params=params,
        cost_estimate=cost(3.5),
        name="partials",
    )(
        *map(
            in_hbm,
            (
                kept_blocks,
                assignment,
                owner_counts,
                inputs_t,
                grad_proj,
                stored_blocks,
                block_scales,
            ),
        )
    )

    far_got = flipped(far_send, 1)
    far_scaled = flipped(scaled, 2)
    far_sums, near_send = pl.pallas_call(
        far_sum_kernel,
        out_shape=(
            jax.ShapeDtypeStruct((message_rows(outer * cap, slab_rows), side), jnp.int16),
            jax.ShapeDtypeStruct(side_shape, jnp.float32),
        ),
        in_specs=[VMEM_SPEC] * 3,
        out_specs=(VMEM_SPEC, VMEM_SPEC),
        compiler_params=params,
        cost_estimate=cost(3.0),
        name="far_sums",
    )(far_keep, far_got, near_send)
    near_got = flipped(near_send, 1)

    pair = stacked("pair", 5.0, far_sums, scaled, far_scaled)
    pairs = [pair] + [stepped(pair, step) for step in range(1, outer)]
    own_sum, *near_sums = pl.pallas_call(
        near_sum_kernel,
        out_shape=[jax.ShapeDtypeStruct(block_shape, jnp.float32)]
        + [jax.ShapeDtypeStruct(message_shape, jnp.int16)] * (outer - 1),
        in_specs=[VMEM_SPEC] * 3,
        out_specs=[VMEM_SPEC] * outer,
        compiler_params=params,
        cost_estimate=cost(0.3),
        name="near_sums",
    )(near_keep, near_got, flipped(far_sums, 2))
    received = [stepped(value, step + 1) for step, value in enumerate(near_sums)]

    for number, group in enumerate((received[:1], received[2:])):
        own_sum = pl.pallas_call(
            add_kernel,
            out_shape=jax.ShapeDtypeStruct(block_shape, jnp.float32),
            in_specs=[VMEM_SPEC] * (1 + len(group)),
            out_specs=VMEM_SPEC,
            compiler_params=params,
            cost_estimate=cost(6.0),
            name="add_%d" % number,
        )(own_sum, *group)
    second = stacked("mine_2", 3.0, near_sums[0], *pairs[2:3])
    others = stacked("mine_3", 3.0, second, *pairs[3:])
    mine = stacked("mine", 0.1, others, pair, pairs[1], second, others)
    other = flipped(mine, 1)

    own_grads, dots = pl.pallas_call(
        functools.partial(owner_sum_kernel, norm),
        out_shape=(
            jax.ShapeDtypeStruct((1,) + block_shape, jnp.float32),
            jax.ShapeDtypeStruct((cap, side), jnp.float32),
        ),
        in_specs=[VMEM_SPEC] * 4,
        out_specs=(VMEM_SPEC, VMEM_SPEC),
        compiler_params=params,
        cost_estimate=cost(6.0),
        name="owner_sums",
    )(scale_rows, stored, own_sum, received[1])
    other_dots = lax.ppermute(dots, "group", [(0, 1), (1, 0)])
    grad_inputs_t, block_grads = pl.pallas_call(
        input_grad_kernel,
        out_shape=(
            jax.ShapeDtypeStruct(inputs_t.shape, jnp.bfloat16),
            jax.ShapeDtypeStruct((1,) + block_shape, jnp.float32),
        ),
        in_specs=[SMEM_SPEC] + [VMEM_SPEC] * 4,
        out_specs=(VMEM_SPEC, VMEM_SPEC),
        scratch_shapes=[pltpu.VMEM(inputs_t.shape, jnp.float32)],
        compiler_params=params,
        cost_estimate=cost(2.0),
        name="input_grads",
    )(table, columns, mine, other, own_grads)
    scale_grads = pl.pallas_call(
        finish_kernel,
        out_shape=jax.ShapeDtypeStruct((1, cap), jnp.float32),
        in_specs=[VMEM_SPEC] * 2 + [HBM_SPEC],
        out_specs=VMEM_SPEC,
        compiler_params=params,
        cost_estimate=cost(0.5),
        name="finish",
    )(dots, other_dots, in_hbm(grad_inputs_t))
    return (grad_inputs_t, block_grads, scale_grads)


def solution(mesh):
    return jax.shard_map(
        on_device,
        mesh=mesh,
        in_specs=(
            P(None, "group", "dp"),
            P(None, None, None, "dp"),
            P("dp", None, "group", None),
            P("dp", None),
            P(),
            P(),
            P(),
        ),
        out_specs=(P(None, "group", "dp"), P("dp", None, "group", None), P("dp", None)),
        check_vma=False,
    )
```

```python
import functools
import math

import jax
import jax.numpy as jnp
from jax import lax
from jax.experimental import pallas as pl
from jax.experimental.pallas import tpu as pltpu
from jax.sharding import PartitionSpec as P

VMEM_LIMIT = 48 * 1024 * 1024
TAIL = 16
UNIT = 2.0**15
SMEM_SPEC = pl.BlockSpec(memory_space=pltpu.SMEM)
VMEM_SPEC = pl.BlockSpec(memory_space=pltpu.VMEM)
ANY_SPEC = pl.BlockSpec(memory_space=pl.ANY)
HBM_SPEC = pl.BlockSpec(memory_space=pltpu.HBM)


def magic_divide(value, divisor, limit):
    shift = 20
    factor = -(-(1 << shift) // divisor)
    assert limit * factor < 1 << 31
    assert all((v * factor) >> shift == v // divisor for v in range(limit))
    return (value * factor) >> shift


def partial_kernel(
    kept_hbm, assign_hbm, counts_hbm, x_hbm, grad_ref, stored_hbm, scales_hbm,
    near_keep, near_send, far_keep, far_send, cols_ref, tab_ref, scaled_ref, stored_ref, scale_rows,
    part_ref, x_ref, scales_ref, kept, assign, counts, slot_ref, sem, index_sems, x_sem
):
    x_copy = pltpu.make_async_copy(x_hbm, x_ref, x_sem)
    index_copies = [
        pltpu.make_async_copy(source, target, index_sems.at[i])
        for i, (source, target) in enumerate(
            (
                (assign_hbm, assign),
                (kept_hbm, kept),
                (counts_hbm, counts),
                (scales_hbm, scales_ref),
                (stored_hbm, stored_ref),
            )
        )
    ]
    for copy in index_copies:
        copy.start()
    x_copy.start()
    keep_count = kept.shape[1]
    hid_blocks = grad_ref.shape[1]
    total = x_ref.shape[0] * hid_blocks
    owners = counts.shape[0]
    entries = assign.shape[0]
    outer, cap = near_keep.shape[:2]
    me = lax.axis_index("dp")
    part_ref[...] = jnp.zeros_like(part_ref)
    for copy in index_copies[:2]:
        copy.wait()

    def fetch_step(p, carry):
        entry = assign[p]
        matrix = jnp.where(entry >= keep_count, 1, 0)
        block = kept[matrix, entry - matrix * keep_count]
        row = magic_divide(block, hid_blocks, total)
        column = block - row * hid_blocks
        pltpu.make_async_copy(grad_ref.at[matrix, column], cols_ref.at[p], sem).start()
        tab_ref[0, p] = row
        return carry

    lax.fori_loop(0, entries, fetch_step, 0, unroll=min(entries, 24))
    for copy in index_copies[2:]:
        copy.wait()

    def owner_step(owner, offset):
        kind = (owner & 3) ^ (me & 3)
        if is_paired(outer):
            step_to = step_from = (owner >> 2) ^ (me >> 2)
        else:
            away = (owner >> 2) - (me >> 2)
            step_to = jnp.where(away < 0, away + outer, away)
            step_from = jnp.where(away > 0, outer - away, -away)
        for c in range(cap):

            @pl.when(c < counts[owner])
            def _():
                p = offset + c
                slot_ref[p] = (kind * outer + step_to) * cap + c
                tab_ref[1, p] = kind
                tab_ref[2, p] = step_from
                tab_ref[3, p] = c

        return offset + counts[owner]

    lax.fori_loop(0, owners, owner_step, 0, unroll=min(owners, 16))
    for c in range(cap):
        scaled = scales_ref[0, c] * stored_ref[0, c].astype(jnp.float32)
        scaled_ref[c] = scaled.astype(jnp.bfloat16)
        scale_rows[c] = jnp.full(scale_rows.shape[1:], scales_ref[0, c], jnp.float32)
    x_copy.wait()
    pltpu.make_async_copy(cols_ref, cols_ref, sem).wait()

    def entry_step(p, carry):
        part_ref[slot_ref[p]] = lax.dot_general(
            x_ref[tab_ref[0, p]],
            cols_ref[p],
            (((1,), (1,)), ((), ())),
            preferred_element_type=jnp.float32,
        )
        return carry

    lax.fori_loop(0, entries, entry_step, 0, unroll=min(entries, 24))
    size = outer * cap
    for kind, ref in enumerate((near_keep, near_send, far_keep, far_send)):
        ref[...] = part_ref[kind * size : (kind + 1) * size].reshape(ref.shape)


def encode(total):
    largest = jnp.max(jnp.abs(total), axis=0, keepdims=True)
    power = jnp.ceil(jnp.log2(jnp.maximum(largest, 2.0**-126)))
    power = jnp.clip(power, -126.0, 126.0)
    level = jnp.floor(total * jnp.exp2(-power) * UNIT + 0.5)
    level = jnp.clip(level, -UNIT, UNIT - 1.0)
    return level.astype(jnp.int32).astype(jnp.int16), power


def message_rows(blocks, slab_rows):
    return blocks * slab_rows + -(-blocks // TAIL) * TAIL


def write_message(totals, out_ref):
    blocks, (slab_rows, side) = len(totals), totals[0].shape
    tail_rows = out_ref.shape[0] - blocks * slab_rows
    tail_row = lax.broadcasted_iota(jnp.int32, (tail_rows, side), 0)
    tail = jnp.zeros((tail_rows, side), jnp.float32)
    for i, total in enumerate(totals):
        level, power = encode(total)
        out_ref[i * slab_rows : (i + 1) * slab_rows] = level
        tail = jnp.where(tail_row == i, power, tail)
    out_ref[blocks * slab_rows :] = tail.astype(jnp.int32).astype(jnp.int16)


def read_message(blocks, slab_rows, ref):
    powers = ref[blocks * slab_rows :].astype(jnp.int32).astype(jnp.float32)
    units = jnp.exp2(powers) * (1.0 / UNIT)
    totals = []
    for i in range(blocks):
        level = ref[i * slab_rows : (i + 1) * slab_rows].astype(jnp.int32)
        totals.append(level.astype(jnp.float32) * units[i : i + 1])
    return totals


def far_sum_kernel(keep_ref, got_ref, near_send, out_ref, near_out):
    near_out[...] = near_send[...]
    outer, cap = keep_ref.shape[:2]
    totals = [keep_ref[k, c] + got_ref[k, c] for k in range(outer) for c in range(cap)]
    write_message(totals, out_ref)


def near_sum_kernel(keep_ref, got_ref, far_ref, *out_refs):
    outer, cap, slab_rows, side = keep_ref.shape
    far = read_message(outer * cap, slab_rows, far_ref)
    for step in range(outer):
        totals = [
            keep_ref[step, c] + got_ref[step, c] + far[step * cap + c] for c in range(cap)
        ]
        if step == 0:
            for c in range(cap):
                out_refs[0][c] = totals[c]
        else:
            write_message(totals, out_refs[step])


def add_kernel(own_ref, *refs):
    *got_refs, out_ref = refs
    cap, slab_rows, side = own_ref.shape
    totals = [own_ref[c] for c in range(cap)]
    for got_ref in got_refs:
        totals = [a + b for a, b in zip(totals, read_message(cap, slab_rows, got_ref))]
    for c in range(cap):
        out_ref[c] = totals[c]


def stack_kernel(*refs):
    *in_refs, _, out_ref = refs
    at = 0
    for in_ref in in_refs:
        if in_ref.ndim < out_ref.ndim:
            out_ref[at] = in_ref[...]
            at += 1
        else:
            out_ref[at : at + in_ref.shape[0]] = in_ref[...]
            at += in_ref.shape[0]


def input_grad_kernel(tab_ref, cols_ref, mine, other, block_ref, out_ref, block_out, acc_ref):
    entries = cols_ref.shape[0]
    block_out[...] = block_ref[...]
    acc_ref[...] = jnp.zeros_like(acc_ref)

    def entry_step(p, carry):
        kind, behind, c = tab_ref[1, p], tab_ref[2, p], tab_ref[3, p]
        block = jnp.where(
            (kind & 1) == 0, mine[behind, kind >> 1, c], other[behind, kind >> 1, c]
        )
        row = tab_ref[0, p]
        acc_ref[row] += jnp.dot(block, cols_ref[p], preferred_element_type=jnp.float32)
        return carry

    lax.fori_loop(0, entries, entry_step, 0, unroll=min(entries, 24))
    out_ref[...] = acc_ref[...].astype(out_ref.dtype)


def owner_sum_kernel(norm, scales_ref, stored_ref, own_ref, *refs):
    got_refs, (block_ref, dots_ref) = refs[:-2], refs[-2:]
    cap, slab_rows, side = stored_ref.shape[1:]
    totals = [own_ref[c] for c in range(cap)]
    for got_ref in got_refs:
        totals = [a + b for a, b in zip(totals, read_message(cap, slab_rows, got_ref))]
    for c in range(cap):
        gradient = totals[c] * norm
        block_ref[0, c] = scales_ref[c, 0:1] * gradient
        dots_ref[c : c + 1, :] = jnp.sum(
            stored_ref[0, c].astype(jnp.float32) * gradient, axis=0, keepdims=True
        )


def finish_kernel(dots_ref, got_ref, grads_ref, scale_out):
    del grads_ref
    total = jnp.sum(dots_ref[...] + got_ref[...], axis=1, keepdims=True)
    cap = total.shape[0]
    row = lax.broadcasted_iota(jnp.int32, (cap, cap), 0)
    column = lax.broadcasted_iota(jnp.int32, (cap, cap), 1)
    scale_out[...] = jnp.sum(jnp.where(row == column, total, 0.0), axis=0, keepdims=True)


def cost(microseconds):
    return pl.CostEstimate(
        flops=int(microseconds * 1_153_000_000), bytes_accessed=int(microseconds * 3_690_000), transcendentals=0
    )


def in_hbm(value):
    return pltpu.with_memory_space_constraint(value, pltpu.HBM)


def flipped(value, bit):
    return lax.ppermute(value, "dp", [(i, i ^ bit) for i in range(lax.axis_size("dp"))])


def is_paired(size):
    return size & (size - 1) == 0


def ahead(places, start, step):
    return start ^ step if is_paired(places) else (start + step) % places


def stepped(value, step):
    size = lax.axis_size("dp")
    return lax.ppermute(
        value, "dp", [(i, ahead(size // 4, i // 4, step) * 4 + i % 4) for i in range(size)]
    )


def stacked(name, estimate, after, *values):
    single = min(value.ndim for value in values)
    count = sum(1 if value.ndim == single else value.shape[0] for value in values)
    shape = (count,) + values[0].shape
    return pl.pallas_call(
        stack_kernel,
        out_shape=jax.ShapeDtypeStruct(shape, values[0].dtype),
        in_specs=[VMEM_SPEC] * len(values) + [ANY_SPEC],
        out_specs=VMEM_SPEC,
        compiler_params=pltpu.CompilerParams(vmem_limit_bytes=VMEM_LIMIT),
        cost_estimate=cost(estimate),
        name=name,
    )(*values, after)


def on_device(
    inputs_t, grad_proj, stored_blocks, block_scales, kept_blocks, assignment, owner_counts
):
    row_blocks, slab_rows, tokens_here = inputs_t.shape
    cap, side = stored_blocks.shape[1], stored_blocks.shape[3]
    entries = assignment.shape[0]
    devices = lax.axis_size("dp")
    outer = devices // 4
    norm = 1.0 / math.sqrt(tokens_here * devices)
    params = pltpu.CompilerParams(vmem_limit_bytes=VMEM_LIMIT)
    block_shape = (cap, slab_rows, side)
    side_shape = (outer, cap, slab_rows, side)
    message_shape = (message_rows(cap, slab_rows), side)

    near_keep, near_send, far_keep, far_send, columns, table, scaled, stored, scale_rows = pl.pallas_call(
        partial_kernel,
        out_shape=[jax.ShapeDtypeStruct(side_shape, jnp.float32)] * 4
        + [
            jax.ShapeDtypeStruct((entries, side, tokens_here), jnp.bfloat16),
            jax.ShapeDtypeStruct((4, entries), jnp.int32),
            jax.ShapeDtypeStruct(block_shape, jnp.bfloat16),
            jax.ShapeDtypeStruct(stored_blocks.shape, jnp.bfloat16),
            jax.ShapeDtypeStruct((cap, 8, side), jnp.float32),
        ],
        in_specs=[HBM_SPEC] * 7,
        out_specs=[VMEM_SPEC] * 5 + [SMEM_SPEC] + [VMEM_SPEC] * 3,
        scratch_shapes=[
            pltpu.VMEM((4 * outer * cap, slab_rows, side), jnp.float32),
            pltpu.VMEM(inputs_t.shape, inputs_t.dtype),
            pltpu.SMEM(block_scales.shape, jnp.float32),
            pltpu.SMEM(kept_blocks.shape, jnp.int32),
            pltpu.SMEM(assignment.shape, jnp.int32),
            pltpu.SMEM(owner_counts.shape, jnp.int32),
            pltpu.SMEM((entries,), jnp.int32),
            pltpu.SemaphoreType.DMA,
            pltpu.SemaphoreType.DMA((5,)),
            pltpu.SemaphoreType.DMA,
        ],
        compiler_params=params,
        cost_estimate=cost(3.5),
        name="partials",
    )(
        *map(
            in_hbm,
            (
                kept_blocks,
                assignment,
                owner_counts,
                inputs_t,
                grad_proj,
                stored_blocks,
                block_scales,
            ),
        )
    )

    far_got = flipped(far_send, 1)
    far_scaled = flipped(scaled, 2)
    far_sums, near_send = pl.pallas_call(
        far_sum_kernel,
        out_shape=(
            jax.ShapeDtypeStruct((message_rows(outer * cap, slab_rows), side), jnp.int16),
            jax.ShapeDtypeStruct(side_shape, jnp.float32),
        ),
        in_specs=[VMEM_SPEC] * 3,
        out_specs=(VMEM_SPEC, VMEM_SPEC),
        compiler_params=params,
        cost_estimate=cost(3.0),
        name="far_sums",
    )(far_keep, far_got, near_send)
    near_got = flipped(near_send, 1)

    pair = stacked("pair", 5.0, far_sums, scaled, far_scaled)
    pairs = [pair] + [stepped(pair, step) for step in range(1, outer)]
    own_sum, *near_sums = pl.pallas_call(
        near_sum_kernel,
        out_shape=[jax.ShapeDtypeStruct(block_shape, jnp.float32)]
        + [jax.ShapeDtypeStruct(message_shape, jnp.int16)] * (outer - 1),
        in_specs=[VMEM_SPEC] * 3,
        out_specs=[VMEM_SPEC] * outer,
        compiler_params=params,
        cost_estimate=cost(0.3),
        name="near_sums",
    )(near_keep, near_got, flipped(far_sums, 2))
    received = [stepped(value, step + 1) for step, value in enumerate(near_sums)]

    for number, group in enumerate((received[2:], received[1:2])):
        own_sum = pl.pallas_call(
            add_kernel,
            out_shape=jax.ShapeDtypeStruct(block_shape, jnp.float32),
            in_specs=[VMEM_SPEC] * (1 + len(group)),
            out_specs=VMEM_SPEC,
            compiler_params=params,
            cost_estimate=cost(6.0),
            name="add_%d" % number,
        )(own_sum, *group)
    second = stacked("mine_2", 3.0, near_sums[0], *pairs[2:3])
    others = stacked("mine_3", 3.0, second, *pairs[3:])
    mine = stacked("mine", 0.1, others, pair, pairs[1], second, others)
    other = flipped(mine, 1)

    own_grads, dots = pl.pallas_call(
        functools.partial(owner_sum_kernel, norm),
        out_shape=(
            jax.ShapeDtypeStruct((1,) + block_shape, jnp.float32),
            jax.ShapeDtypeStruct((cap, side), jnp.float32),
        ),
        in_specs=[VMEM_SPEC] * 4,
        out_specs=(VMEM_SPEC, VMEM_SPEC),
        compiler_params=params,
        cost_estimate=cost(6.0),
        name="owner_sums",
    )(scale_rows, stored, own_sum, received[0])
    other_dots = lax.ppermute(dots, "group", [(0, 1), (1, 0)])
    grad_inputs_t, block_grads = pl.pallas_call(
        input_grad_kernel,
        out_shape=(
            jax.ShapeDtypeStruct(inputs_t.shape, jnp.bfloat16),
            jax.ShapeDtypeStruct((1,) + block_shape, jnp.float32),
        ),
        in_specs=[SMEM_SPEC] + [VMEM_SPEC] * 4,
        out_specs=(VMEM_SPEC, VMEM_SPEC),
        scratch_shapes=[pltpu.VMEM(inputs_t.shape, jnp.float32)],
        compiler_params=params,
        cost_estimate=cost(2.0),
        name="input_grads",
    )(table, columns, mine, other, own_grads)
    scale_grads = pl.pallas_call(
        finish_kernel,
        out_shape=jax.ShapeDtypeStruct((1, cap), jnp.float32),
        in_specs=[VMEM_SPEC] * 2 + [HBM_SPEC],
        out_specs=VMEM_SPEC,
        compiler_params=params,
        cost_estimate=cost(0.5),
        name="finish",
    )(dots, other_dots, in_hbm(grad_inputs_t))
    return (grad_inputs_t, block_grads, scale_grads)


def solution(mesh):
    return jax.shard_map(
        on_device,
        mesh=mesh,
        in_specs=(
            P(None, "group", "dp"),
            P(None, None, None, "dp"),
            P("dp", None, "group", None),
            P("dp", None),
            P(),
            P(),
            P(),
        ),
        out_specs=(P(None, "group", "dp"), P("dp", None, "group", None), P("dp", None)),
        check_vma=False,
    )
```

```python
import functools
import math

import jax
import jax.numpy as jnp
from jax import lax
from jax.experimental import pallas as pl
from jax.experimental.pallas import tpu as pltpu
from jax.sharding import PartitionSpec as P

VMEM_LIMIT = 48 * 1024 * 1024
TAIL = 16
UNIT = 2.0**15
SMEM_SPEC = pl.BlockSpec(memory_space=pltpu.SMEM)
VMEM_SPEC = pl.BlockSpec(memory_space=pltpu.VMEM)
ANY_SPEC = pl.BlockSpec(memory_space=pl.ANY)
HBM_SPEC = pl.BlockSpec(memory_space=pltpu.HBM)


def magic_divide(value, divisor, limit):
    shift = 20
    factor = -(-(1 << shift) // divisor)
    assert limit * factor < 1 << 31
    assert all((v * factor) >> shift == v // divisor for v in range(limit))
    return (value * factor) >> shift


def slot_blocks(kinds, refs, me, tab_ref, span_ref, x_ref, cols_ref):
    outer, cap = refs[0].shape[:2]
    entries = cols_ref.shape[0]
    home = me >> 2

    def step_blocks(step, carry):
        place = home ^ step if is_paired(outer) else lax.rem(home + step, outer)
        for kind, ref in zip(kinds, refs):
            owner = place * 4 + ((me & 3) ^ kind)
            for c in range(cap):
                p = jnp.minimum(span_ref[0, owner] + c, entries - 1)
                block = lax.dot_general(
                    x_ref[tab_ref[0, p]],
                    cols_ref[p],
                    (((1,), (1,)), ((), ())),
                    preferred_element_type=jnp.float32,
                )
                ref[step, c] = jnp.where(c < span_ref[1, owner], block, 0.0)
        return carry

    lax.fori_loop(0, outer, step_blocks, 0, unroll=min(outer, 4))


def partial_kernel(
    kept_hbm, assign_hbm, counts_hbm, x_hbm, grad_ref, stored_hbm, scales_hbm,
    far_keep, far_send, x_ref, cols_ref, tab_ref, span_ref, scaled_ref, stored_ref, scale_rows,
    scales_ref, kept, assign, counts, sem, index_sems, x_sem
):
    x_copy = pltpu.make_async_copy(x_hbm, x_ref, x_sem)
    index_copies = [
        pltpu.make_async_copy(source, target, index_sems.at[i])
        for i, (source, target) in enumerate(
            (
                (assign_hbm, assign),
                (kept_hbm, kept),
                (counts_hbm, counts),
                (scales_hbm, scales_ref),
                (stored_hbm, stored_ref),
            )
        )
    ]
    for copy in index_copies:
        copy.start()
    x_copy.start()
    keep_count = kept.shape[1]
    hid_blocks = grad_ref.shape[1]
    total = x_ref.shape[0] * hid_blocks
    owners = counts.shape[0]
    entries = assign.shape[0]
    outer, cap = far_keep.shape[:2]
    me = lax.axis_index("dp")
    for copy in index_copies[:2]:
        copy.wait()

    def fetch_step(p, carry):
        entry = assign[p]
        matrix = jnp.where(entry >= keep_count, 1, 0)
        block = kept[matrix, entry - matrix * keep_count]
        row = magic_divide(block, hid_blocks, total)
        column = block - row * hid_blocks
        pltpu.make_async_copy(grad_ref.at[matrix, column], cols_ref.at[p], sem).start()
        tab_ref[0, p] = row
        return carry

    lax.fori_loop(0, entries, fetch_step, 0, unroll=min(entries, 24))
    for copy in index_copies[2:]:
        copy.wait()

    def owner_step(owner, offset):
        kind = (owner & 3) ^ (me & 3)
        if is_paired(outer):
            step_from = (owner >> 2) ^ (me >> 2)
        else:
            away = (owner >> 2) - (me >> 2)
            step_from = jnp.where(away > 0, outer - away, -away)
        count = counts[owner]
        span_ref[0, owner] = offset
        span_ref[1, owner] = count
        for c in range(cap):

            @pl.when(c < count)
            def _():
                p = offset + c
                tab_ref[1, p] = kind
                tab_ref[2, p] = step_from
                tab_ref[3, p] = c

        return offset + count

    lax.fori_loop(0, owners, owner_step, 0, unroll=min(owners, 16))
    for c in range(cap):
        scaled = scales_ref[0, c] * stored_ref[0, c].astype(jnp.float32)
        scaled_ref[c] = scaled.astype(jnp.bfloat16)
        scale_rows[c] = jnp.full(scale_rows.shape[1:], scales_ref[0, c], jnp.float32)
    x_copy.wait()
    pltpu.make_async_copy(cols_ref, cols_ref, sem).wait()
    slot_blocks((2, 3), (far_keep, far_send), me, tab_ref, span_ref, x_ref, cols_ref)


def near_partial_kernel(tab_ref, span_ref, x_ref, cols_ref, near_keep, near_send):
    me = lax.axis_index("dp")
    slot_blocks((0, 1), (near_keep, near_send), me, tab_ref, span_ref, x_ref, cols_ref)


def encode(total):
    largest = jnp.max(jnp.abs(total), axis=0, keepdims=True)
    power = jnp.ceil(jnp.log2(jnp.maximum(largest, 2.0**-126)))
    power = jnp.clip(power, -126.0, 126.0)
    level = jnp.floor(total * jnp.exp2(-power) * UNIT + 0.5)
    level = jnp.clip(level, -UNIT, UNIT - 1.0)
    return level.astype(jnp.int32).astype(jnp.int16), power


def message_rows(blocks, slab_rows):
    return blocks * slab_rows + -(-blocks // TAIL) * TAIL


def write_message(totals, out_ref):
    blocks, (slab_rows, side) = len(totals), totals[0].shape
    tail_rows = out_ref.shape[0] - blocks * slab_rows
    tail_row = lax.broadcasted_iota(jnp.int32, (tail_rows, side), 0)
    tail = jnp.zeros((tail_rows, side), jnp.float32)
    for i, total in enumerate(totals):
        level, power = encode(total)
        out_ref[i * slab_rows : (i + 1) * slab_rows] = level
        tail = jnp.where(tail_row == i, power, tail)
    out_ref[blocks * slab_rows :] = tail.astype(jnp.int32).astype(jnp.int16)


def read_message(blocks, slab_rows, ref):
    powers = ref[blocks * slab_rows :].astype(jnp.int32).astype(jnp.float32)
    units = jnp.exp2(powers) * (1.0 / UNIT)
    totals = []
    for i in range(blocks):
        level = ref[i * slab_rows : (i + 1) * slab_rows].astype(jnp.int32)
        totals.append(level.astype(jnp.float32) * units[i : i + 1])
    return totals


def far_sum_kernel(keep_ref, got_ref, near_send, out_ref, near_out):
    near_out[...] = near_send[...]
    outer, cap = keep_ref.shape[:2]
    totals = [keep_ref[k, c] + got_ref[k, c] for k in range(outer) for c in range(cap)]
    write_message(totals, out_ref)


def near_sum_kernel(keep_ref, got_ref, far_ref, *out_refs):
    outer, cap, slab_rows, side = keep_ref.shape
    far = read_message(outer * cap, slab_rows, far_ref)
    for step in range(outer):
        totals = [
            keep_ref[step, c] + got_ref[step, c] + far[step * cap + c] for c in range(cap)
        ]
        if step == 0:
            for c in range(cap):
                out_refs[0][c] = totals[c]
        else:
            write_message(totals, out_refs[step])


def add_kernel(own_ref, *refs):
    *got_refs, out_ref = refs
    cap, slab_rows, side = own_ref.shape
    totals = [own_ref[c] for c in range(cap)]
    for got_ref in got_refs:
        totals = [a + b for a, b in zip(totals, read_message(cap, slab_rows, got_ref))]
    for c in range(cap):
        out_ref[c] = totals[c]


def stack_kernel(*refs):
    *in_refs, _, out_ref = refs
    at = 0
    for in_ref in in_refs:
        if in_ref.ndim < out_ref.ndim:
            out_ref[at] = in_ref[...]
            at += 1
        else:
            out_ref[at : at + in_ref.shape[0]] = in_ref[...]
            at += in_ref.shape[0]


def input_grad_kernel(tab_ref, cols_ref, mine, other, block_ref, out_ref, block_out, acc_ref):
    entries = cols_ref.shape[0]
    block_out[...] = block_ref[...]
    acc_ref[...] = jnp.zeros_like(acc_ref)

    def entry_step(p, carry):
        kind, behind, c = tab_ref[1, p], tab_ref[2, p], tab_ref[3, p]
        block = jnp.where(
            (kind & 1) == 0, mine[behind, kind >> 1, c], other[behind, kind >> 1, c]
        )
        row = tab_ref[0, p]
        acc_ref[row] += jnp.dot(block, cols_ref[p], preferred_element_type=jnp.float32)
        return carry

    lax.fori_loop(0, entries, entry_step, 0, unroll=min(entries, 24))
    out_ref[...] = acc_ref[...].astype(out_ref.dtype)


def owner_sum_kernel(norm, scales_ref, stored_ref, own_ref, *refs):
    got_refs, (block_ref, dots_ref) = refs[:-2], refs[-2:]
    cap, slab_rows, side = stored_ref.shape[1:]
    totals = [own_ref[c] for c in range(cap)]
    for got_ref in got_refs:
        totals = [a + b for a, b in zip(totals, read_message(cap, slab_rows, got_ref))]
    for c in range(cap):
        gradient = totals[c] * norm
        block_ref[0, c] = scales_ref[c, 0:1] * gradient
        dots_ref[c : c + 1, :] = jnp.sum(
            stored_ref[0, c].astype(jnp.float32) * gradient, axis=0, keepdims=True
        )


def finish_kernel(dots_ref, got_ref, grads_ref, scale_out):
    del grads_ref
    total = jnp.sum(dots_ref[...] + got_ref[...], axis=1, keepdims=True)
    cap = total.shape[0]
    row = lax.broadcasted_iota(jnp.int32, (cap, cap), 0)
    column = lax.broadcasted_iota(jnp.int32, (cap, cap), 1)
    scale_out[...] = jnp.sum(jnp.where(row == column, total, 0.0), axis=0, keepdims=True)


def cost(microseconds):
    return pl.CostEstimate(
        flops=int(microseconds * 1_153_000_000), bytes_accessed=int(microseconds * 3_690_000), transcendentals=0
    )


def in_hbm(value):
    return pltpu.with_memory_space_constraint(value, pltpu.HBM)


def flipped(value, bit):
    return lax.ppermute(value, "dp", [(i, i ^ bit) for i in range(lax.axis_size("dp"))])


def is_paired(size):
    return size & (size - 1) == 0


def ahead(places, start, step):
    return start ^ step if is_paired(places) else (start + step) % places


def stepped(value, step):
    size = lax.axis_size("dp")
    return lax.ppermute(
        value, "dp", [(i, ahead(size // 4, i // 4, step) * 4 + i % 4) for i in range(size)]
    )


def stacked(name, estimate, after, *values):
    single = min(value.ndim for value in values)
    count = sum(1 if value.ndim == single else value.shape[0] for value in values)
    shape = (count,) + values[0].shape
    return pl.pallas_call(
        stack_kernel,
        out_shape=jax.ShapeDtypeStruct(shape, values[0].dtype),
        in_specs=[VMEM_SPEC] * len(values) + [ANY_SPEC],
        out_specs=VMEM_SPEC,
        compiler_params=pltpu.CompilerParams(vmem_limit_bytes=VMEM_LIMIT),
        cost_estimate=cost(estimate),
        name=name,
    )(*values, after)


def on_device(
    inputs_t, grad_proj, stored_blocks, block_scales, kept_blocks, assignment, owner_counts
):
    row_blocks, slab_rows, tokens_here = inputs_t.shape
    cap, side = stored_blocks.shape[1], stored_blocks.shape[3]
    entries = assignment.shape[0]
    devices = lax.axis_size("dp")
    outer = devices // 4
    norm = 1.0 / math.sqrt(tokens_here * devices)
    params = pltpu.CompilerParams(vmem_limit_bytes=VMEM_LIMIT)
    block_shape = (cap, slab_rows, side)
    side_shape = (outer, cap, slab_rows, side)
    message_shape = (message_rows(cap, slab_rows), side)

    side_sums = jax.ShapeDtypeStruct(side_shape, jnp.float32)
    far_keep, far_send, rows, columns, table, spans, scaled, stored, scale_rows = pl.pallas_call(
        partial_kernel,
        out_shape=[
            side_sums,
            side_sums,
            jax.ShapeDtypeStruct(inputs_t.shape, inputs_t.dtype),
            jax.ShapeDtypeStruct((entries, side, tokens_here), jnp.bfloat16),
            jax.ShapeDtypeStruct((4, entries), jnp.int32),
            jax.ShapeDtypeStruct((2,) + owner_counts.shape, jnp.int32),
            jax.ShapeDtypeStruct(block_shape, jnp.bfloat16),
            jax.ShapeDtypeStruct(stored_blocks.shape, jnp.bfloat16),
            jax.ShapeDtypeStruct((cap, 8, side), jnp.float32),
        ],
        in_specs=[HBM_SPEC] * 7,
        out_specs=[VMEM_SPEC] * 4 + [SMEM_SPEC] * 2 + [VMEM_SPEC] * 3,
        scratch_shapes=[
            pltpu.SMEM(block_scales.shape, jnp.float32),
            pltpu.SMEM(kept_blocks.shape, jnp.int32),
            pltpu.SMEM(assignment.shape, jnp.int32),
            pltpu.SMEM(owner_counts.shape, jnp.int32),
            pltpu.SemaphoreType.DMA,
            pltpu.SemaphoreType.DMA((5,)),
            pltpu.SemaphoreType.DMA,
        ],
        compiler_params=params,
        cost_estimate=cost(3.5),
        name="partials",
    )(
        *map(
            in_hbm,
            (
                kept_blocks,
                assignment,
                owner_counts,
                inputs_t,
                grad_proj,
                stored_blocks,
                block_scales,
            ),
        )
    )
    near_keep, near_send = pl.pallas_call(
        near_partial_kernel,
        out_shape=[side_sums, side_sums],
        in_specs=[SMEM_SPEC] * 2 + [VMEM_SPEC] * 2,
        out_specs=[VMEM_SPEC] * 2,
        compiler_params=params,
        cost_estimate=cost(1.0),
        name="near_partials",
    )(table, spans, rows, columns)

    far_got = flipped(far_send, 1)
    far_scaled = flipped(scaled, 2)
    far_sums, near_send = pl.pallas_call(
        far_sum_kernel,
        out_shape=(
            jax.ShapeDtypeStruct((message_rows(outer * cap, slab_rows), side), jnp.int16),
            jax.ShapeDtypeStruct(side_shape, jnp.float32),
        ),
        in_specs=[VMEM_SPEC] * 3,
        out_specs=(VMEM_SPEC, VMEM_SPEC),
        compiler_params=params,
        cost_estimate=cost(3.0),
        name="far_sums",
    )(far_keep, far_got, near_send)
    near_got = flipped(near_send, 1)

    pair = stacked("pair", 5.0, far_sums, scaled, far_scaled)
    pairs = [pair] + [stepped(pair, step) for step in range(1, outer)]
    own_sum, *near_sums = pl.pallas_call(
        near_sum_kernel,
        out_shape=[jax.ShapeDtypeStruct(block_shape, jnp.float32)]
        + [jax.ShapeDtypeStruct(message_shape, jnp.int16)] * (outer - 1),
        in_specs=[VMEM_SPEC] * 3,
        out_specs=[VMEM_SPEC] * outer,
        compiler_params=params,
        cost_estimate=cost(0.3),
        name="near_sums",
    )(near_keep, near_got, flipped(far_sums, 2))
    received = [stepped(value, step + 1) for step, value in enumerate(near_sums)]

    for number, group in enumerate((received[2:], received[1:2])):
        own_sum = pl.pallas_call(
            add_kernel,
            out_shape=jax.ShapeDtypeStruct(block_shape, jnp.float32),
            in_specs=[VMEM_SPEC] * (1 + len(group)),
            out_specs=VMEM_SPEC,
            compiler_params=params,
            cost_estimate=cost(6.0),
            name="add_%d" % number,
        )(own_sum, *group)
    second = stacked("mine_2", 3.0, near_sums[0], *pairs[2:3])
    others = stacked("mine_3", 3.0, second, *pairs[3:])
    mine = stacked("mine", 0.1, others, pair, pairs[1], second, others)
    other = flipped(mine, 1)

    own_grads, dots = pl.pallas_call(
        functools.partial(owner_sum_kernel, norm),
        out_shape=(
            jax.ShapeDtypeStruct((1,) + block_shape, jnp.float32),
            jax.ShapeDtypeStruct((cap, side), jnp.float32),
        ),
        in_specs=[VMEM_SPEC] * 4,
        out_specs=(VMEM_SPEC, VMEM_SPEC),
        compiler_params=params,
        cost_estimate=cost(6.0),
        name="owner_sums",
    )(scale_rows, stored, own_sum, received[0])
    other_dots = lax.ppermute(dots, "group", [(0, 1), (1, 0)])
    grad_inputs_t, block_grads = pl.pallas_call(
        input_grad_kernel,
        out_shape=(
            jax.ShapeDtypeStruct(inputs_t.shape, jnp.bfloat16),
            jax.ShapeDtypeStruct((1,) + block_shape, jnp.float32),
        ),
        in_specs=[SMEM_SPEC] + [VMEM_SPEC] * 4,
        out_specs=(VMEM_SPEC, VMEM_SPEC),
        scratch_shapes=[pltpu.VMEM(inputs_t.shape, jnp.float32)],
        compiler_params=params,
        cost_estimate=cost(2.0),
        name="input_grads",
    )(table, columns, mine, other, own_grads)
    scale_grads = pl.pallas_call(
        finish_kernel,
        out_shape=jax.ShapeDtypeStruct((1, cap), jnp.float32),
        in_specs=[VMEM_SPEC] * 2 + [HBM_SPEC],
        out_specs=VMEM_SPEC,
        compiler_params=params,
        cost_estimate=cost(0.5),
        name="finish",
    )(dots, other_dots, in_hbm(grad_inputs_t))
    return (grad_inputs_t, block_grads, scale_grads)


def solution(mesh):
    return jax.shard_map(
        on_device,
        mesh=mesh,
        in_specs=(
            P(None, "group", "dp"),
            P(None, None, None, "dp"),
            P("dp", None, "group", None),
            P("dp", None),
            P(),
            P(),
            P(),
        ),
        out_specs=(P(None, "group", "dp"), P("dp", None, "group", None), P("dp", None)),
        check_vma=False,
    )
```

```python
import functools
import math

import jax
import jax.numpy as jnp
from jax import lax
from jax.experimental import pallas as pl
from jax.experimental.pallas import tpu as pltpu
from jax.sharding import PartitionSpec as P

VMEM_LIMIT = 48 * 1024 * 1024
TAIL = 16
UNIT = 2.0**15
SMEM_SPEC = pl.BlockSpec(memory_space=pltpu.SMEM)
VMEM_SPEC = pl.BlockSpec(memory_space=pltpu.VMEM)
ANY_SPEC = pl.BlockSpec(memory_space=pl.ANY)
HBM_SPEC = pl.BlockSpec(memory_space=pltpu.HBM)


def magic_divide(value, divisor, limit):
    shift = 20
    factor = -(-(1 << shift) // divisor)
    assert limit * factor < 1 << 31
    assert all((v * factor) >> shift == v // divisor for v in range(limit))
    return (value * factor) >> shift


def partial_kernel(
    kept_hbm, assign_hbm, counts_hbm, x_hbm, grad_ref, stored_hbm, scales_hbm,
    near_keep, near_send, far_keep, far_send, cols_ref, tab_ref, scaled_ref, stored_ref, scale_rows,
    part_ref, x_ref, scales_ref, kept, assign, counts, slot_ref, sem, index_sems, x_sem
):
    x_copy = pltpu.make_async_copy(x_hbm, x_ref, x_sem)
    index_copies = [
        pltpu.make_async_copy(source, target, index_sems.at[i])
        for i, (source, target) in enumerate(
            (
                (assign_hbm, assign),
                (kept_hbm, kept),
                (counts_hbm, counts),
                (scales_hbm, scales_ref),
                (stored_hbm, stored_ref),
            )
        )
    ]
    for copy in index_copies:
        copy.start()
    x_copy.start()
    keep_count = kept.shape[1]
    hid_blocks = grad_ref.shape[1]
    total = x_ref.shape[0] * hid_blocks
    owners = counts.shape[0]
    entries = assign.shape[0]
    outer, cap = near_keep.shape[:2]
    me = lax.axis_index("dp")
    part_ref[...] = jnp.zeros_like(part_ref)
    for copy in index_copies[:2]:
        copy.wait()

    def fetch_step(p, carry):
        entry = assign[p]
        matrix = jnp.where(entry >= keep_count, 1, 0)
        block = kept[matrix, entry - matrix * keep_count]
        row = magic_divide(block, hid_blocks, total)
        column = block - row * hid_blocks
        pltpu.make_async_copy(grad_ref.at[matrix, column], cols_ref.at[p], sem).start()
        tab_ref[0, p] = row
        return carry

    lax.fori_loop(0, entries, fetch_step, 0, unroll=min(entries, 24))
    for copy in index_copies[2:]:
        copy.wait()

    def owner_step(owner, offset):
        kind = (owner & 3) ^ (me & 3)
        if is_paired(outer):
            step_to = step_from = (owner >> 2) ^ (me >> 2)
        else:
            away = (owner >> 2) - (me >> 2)
            step_to = jnp.where(away < 0, away + outer, away)
            step_from = jnp.where(away > 0, outer - away, -away)
        split = step_to >= 2
        summing = jnp.where(split, 1 - (step_to & 1), owner & 1)
        place = jnp.where(split, (step_to & ~1) + (owner & 1), step_to)
        part = (kind & 2) | (summing ^ (me & 1))
        for c in range(cap):

            @pl.when(c < counts[owner])
            def _():
                p = offset + c
                slot_ref[p] = (part * outer + place) * cap + c
                tab_ref[1, p] = kind
                tab_ref[2, p] = step_from
                tab_ref[3, p] = c

        return offset + counts[owner]

    lax.fori_loop(0, owners, owner_step, 0, unroll=min(owners, 16))
    for c in range(cap):
        scaled = scales_ref[0, c] * stored_ref[0, c].astype(jnp.float32)
        scaled_ref[c] = scaled.astype(jnp.bfloat16)
        scale_rows[c] = jnp.full(scale_rows.shape[1:], scales_ref[0, c], jnp.float32)
    x_copy.wait()
    pltpu.make_async_copy(cols_ref, cols_ref, sem).wait()

    def entry_step(p, carry):
        part_ref[slot_ref[p]] = lax.dot_general(
            x_ref[tab_ref[0, p]],
            cols_ref[p],
            (((1,), (1,)), ((), ())),
            preferred_element_type=jnp.float32,
        )
        return carry

    lax.fori_loop(0, entries, entry_step, 0, unroll=min(entries, 24))
    size = outer * cap
    for kind, ref in enumerate((near_keep, near_send, far_keep, far_send)):
        ref[...] = part_ref[kind * size : (kind + 1) * size].reshape(ref.shape)


def encode(total):
    largest = jnp.max(jnp.abs(total), axis=0, keepdims=True)
    power = jnp.ceil(jnp.log2(jnp.maximum(largest, 2.0**-126)))
    power = jnp.clip(power, -126.0, 126.0)
    level = jnp.floor(total * jnp.exp2(-power) * UNIT + 0.5)
    level = jnp.clip(level, -UNIT, UNIT - 1.0)
    return level.astype(jnp.int32).astype(jnp.int16), power


def message_rows(blocks, slab_rows):
    return blocks * slab_rows + -(-blocks // TAIL) * TAIL


def write_message(totals, out_ref):
    blocks, (slab_rows, side) = len(totals), totals[0].shape
    tail_rows = out_ref.shape[0] - blocks * slab_rows
    tail_row = lax.broadcasted_iota(jnp.int32, (tail_rows, side), 0)
    tail = jnp.zeros((tail_rows, side), jnp.float32)
    for i, total in enumerate(totals):
        level, power = encode(total)
        out_ref[i * slab_rows : (i + 1) * slab_rows] = level
        tail = jnp.where(tail_row == i, power, tail)
    out_ref[blocks * slab_rows :] = tail.astype(jnp.int32).astype(jnp.int16)


def read_message(blocks, slab_rows, ref):
    powers = ref[blocks * slab_rows :].astype(jnp.int32).astype(jnp.float32)
    units = jnp.exp2(powers) * (1.0 / UNIT)
    totals = []
    for i in range(blocks):
        level = ref[i * slab_rows : (i + 1) * slab_rows].astype(jnp.int32)
        totals.append(level.astype(jnp.float32) * units[i : i + 1])
    return totals


def far_sum_kernel(keep_ref, got_ref, near_send, out_ref, near_out):
    near_out[...] = near_send[...]
    outer, cap = keep_ref.shape[:2]
    totals = [keep_ref[k, c] + got_ref[k, c] for k in range(outer) for c in range(cap)]
    write_message(totals, out_ref)


def near_sum_kernel(keep_ref, got_ref, far_ref, own_ref, *out_refs):
    outer, cap, slab_rows, side = keep_ref.shape
    far = read_message(outer * cap, slab_rows, far_ref)

    def totals(places):
        return [keep_ref[k, c] + got_ref[k, c] + far[k * cap + c] for k in places for c in range(cap)]

    for c, total in enumerate(totals([0])):
        own_ref[c] = total
    write_message(totals([1]), out_refs[0])
    for i, out_ref in enumerate(out_refs[1:]):
        write_message(totals([2 * i + 2, 2 * i + 3]), out_ref)


def split_kernel(own_ref, *refs):
    *got_refs, mine_ref, other_ref = refs
    cap, slab_rows, side = own_ref.shape
    first_core = (lax.axis_index("dp") & 1) == 0
    sums = [[own_ref[c] for c in range(cap)], [jnp.zeros((slab_rows, side), jnp.float32)] * cap]
    for got_ref in got_refs:
        blocks = read_message(2 * cap, slab_rows, got_ref)
        for c in range(cap):
            sums[0][c] = sums[0][c] + jnp.where(first_core, blocks[c], blocks[cap + c])
            sums[1][c] = sums[1][c] + jnp.where(first_core, blocks[cap + c], blocks[c])
    for c in range(cap):
        mine_ref[c] = sums[0][c]
        other_ref[c] = sums[1][c]


def stack_kernel(*refs):
    *in_refs, _, out_ref = refs
    at = 0
    for in_ref in in_refs:
        if in_ref.ndim < out_ref.ndim:
            out_ref[at] = in_ref[...]
            at += 1
        else:
            out_ref[at : at + in_ref.shape[0]] = in_ref[...]
            at += in_ref.shape[0]


def input_grad_kernel(tab_ref, cols_ref, mine, other, block_ref, out_ref, block_out, acc_ref):
    entries = cols_ref.shape[0]
    block_out[...] = block_ref[...]
    acc_ref[...] = jnp.zeros_like(acc_ref)

    def entry_step(p, carry):
        kind, behind, c = tab_ref[1, p], tab_ref[2, p], tab_ref[3, p]
        block = jnp.where(
            (kind & 1) == 0, mine[behind, kind >> 1, c], other[behind, kind >> 1, c]
        )
        row = tab_ref[0, p]
        acc_ref[row] += jnp.dot(block, cols_ref[p], preferred_element_type=jnp.float32)
        return carry

    lax.fori_loop(0, entries, entry_step, 0, unroll=min(entries, 24))
    out_ref[...] = acc_ref[...].astype(out_ref.dtype)


def owner_sum_kernel(norm, scales_ref, stored_ref, own_ref, other_ref, *refs):
    got_refs, (block_ref, dots_ref) = refs[:-2], refs[-2:]
    cap, slab_rows, side = stored_ref.shape[1:]
    totals = [own_ref[c] + other_ref[c] for c in range(cap)]
    for got_ref in got_refs:
        totals = [a + b for a, b in zip(totals, read_message(cap, slab_rows, got_ref))]
    for c in range(cap):
        gradient = totals[c] * norm
        block_ref[0, c] = scales_ref[c, 0:1] * gradient
        dots_ref[c : c + 1, :] = jnp.sum(
            stored_ref[0, c].astype(jnp.float32) * gradient, axis=0, keepdims=True
        )


def finish_kernel(dots_ref, got_ref, grads_ref, scale_out):
    del grads_ref
    total = jnp.sum(dots_ref[...] + got_ref[...], axis=1, keepdims=True)
    cap = total.shape[0]
    row = lax.broadcasted_iota(jnp.int32, (cap, cap), 0)
    column = lax.broadcasted_iota(jnp.int32, (cap, cap), 1)
    scale_out[...] = jnp.sum(jnp.where(row == column, total, 0.0), axis=0, keepdims=True)


def cost(microseconds):
    return pl.CostEstimate(
        flops=int(microseconds * 1_153_000_000), bytes_accessed=int(microseconds * 3_690_000), transcendentals=0
    )


def in_hbm(value):
    return pltpu.with_memory_space_constraint(value, pltpu.HBM)


def flipped(value, bit):
    return lax.ppermute(value, "dp", [(i, i ^ bit) for i in range(lax.axis_size("dp"))])


def is_paired(size):
    return size & (size - 1) == 0


def ahead(places, start, step):
    return start ^ step if is_paired(places) else (start + step) % places


def stepped(value, step, second_core_step=None):
    size = lax.axis_size("dp")
    steps = (step, step if second_core_step is None else second_core_step)
    return lax.ppermute(
        value,
        "dp",
        [(i, ahead(size // 4, i // 4, steps[i % 2]) * 4 + i % 4) for i in range(size)],
    )


def stacked(name, estimate, after, *values):
    single = min(value.ndim for value in values)
    count = sum(1 if value.ndim == single else value.shape[0] for value in values)
    shape = (count,) + values[0].shape
    return pl.pallas_call(
        stack_kernel,
        out_shape=jax.ShapeDtypeStruct(shape, values[0].dtype),
        in_specs=[VMEM_SPEC] * len(values) + [ANY_SPEC],
        out_specs=VMEM_SPEC,
        compiler_params=pltpu.CompilerParams(vmem_limit_bytes=VMEM_LIMIT),
        cost_estimate=cost(estimate),
        name=name,
    )(*values, after)


def on_device(
    inputs_t, grad_proj, stored_blocks, block_scales, kept_blocks, assignment, owner_counts
):
    row_blocks, slab_rows, tokens_here = inputs_t.shape
    cap, side = stored_blocks.shape[1], stored_blocks.shape[3]
    entries = assignment.shape[0]
    devices = lax.axis_size("dp")
    outer = devices // 4
    norm = 1.0 / math.sqrt(tokens_here * devices)
    params = pltpu.CompilerParams(vmem_limit_bytes=VMEM_LIMIT)
    block_shape = (cap, slab_rows, side)
    side_shape = (outer, cap, slab_rows, side)
    message_shape = (message_rows(cap, slab_rows), side)

    near_keep, near_send, far_keep, far_send, columns, table, scaled, stored, scale_rows = pl.pallas_call(
        partial_kernel,
        out_shape=[jax.ShapeDtypeStruct(side_shape, jnp.float32)] * 4
        + [
            jax.ShapeDtypeStruct((entries, side, tokens_here), jnp.bfloat16),
            jax.ShapeDtypeStruct((4, entries), jnp.int32),
            jax.ShapeDtypeStruct(block_shape, jnp.bfloat16),
            jax.ShapeDtypeStruct(stored_blocks.shape, jnp.bfloat16),
            jax.ShapeDtypeStruct((cap, 8, side), jnp.float32),
        ],
        in_specs=[HBM_SPEC] * 7,
        out_specs=[VMEM_SPEC] * 5 + [SMEM_SPEC] + [VMEM_SPEC] * 3,
        scratch_shapes=[
            pltpu.VMEM((4 * outer * cap, slab_rows, side), jnp.float32),
            pltpu.VMEM(inputs_t.shape, inputs_t.dtype),
            pltpu.SMEM(block_scales.shape, jnp.float32),
            pltpu.SMEM(kept_blocks.shape, jnp.int32),
            pltpu.SMEM(assignment.shape, jnp.int32),
            pltpu.SMEM(owner_counts.shape, jnp.int32),
            pltpu.SMEM((entries,), jnp.int32),
            pltpu.SemaphoreType.DMA,
            pltpu.SemaphoreType.DMA((5,)),
            pltpu.SemaphoreType.DMA,
        ],
        compiler_params=params,
        cost_estimate=cost(3.5),
        name="partials",
    )(
        *map(
            in_hbm,
            (
                kept_blocks,
                assignment,
                owner_counts,
                inputs_t,
                grad_proj,
                stored_blocks,
                block_scales,
            ),
        )
    )

    far_got = flipped(far_send, 1)
    far_scaled = flipped(scaled, 2)
    far_sums, near_send = pl.pallas_call(
        far_sum_kernel,
        out_shape=(
            jax.ShapeDtypeStruct((message_rows(outer * cap, slab_rows), side), jnp.int16),
            jax.ShapeDtypeStruct(side_shape, jnp.float32),
        ),
        in_specs=[VMEM_SPEC] * 3,
        out_specs=(VMEM_SPEC, VMEM_SPEC),
        compiler_params=params,
        cost_estimate=cost(3.0),
        name="far_sums",
    )(far_keep, far_got, near_send)
    near_got = flipped(near_send, 1)

    pair = stacked("pair", 5.0, far_sums, scaled, far_scaled)
    pairs = [pair] + [stepped(pair, step) for step in range(1, outer)]
    message = jax.ShapeDtypeStruct(message_shape, jnp.int16)
    chip_message = jax.ShapeDtypeStruct((message_rows(2 * cap, slab_rows), side), jnp.int16)
    chip_messages = outer // 2 - 1
    own_sum, *near_sums = pl.pallas_call(
        near_sum_kernel,
        out_shape=[jax.ShapeDtypeStruct(block_shape, jnp.float32), message]
        + [chip_message] * chip_messages,
        in_specs=[VMEM_SPEC] * 3,
        out_specs=[VMEM_SPEC] * (2 + chip_messages),
        compiler_params=params,
        cost_estimate=cost(0.3),
        name="near_sums",
    )(near_keep, near_got, flipped(far_sums, 2))
    neighbour = stepped(near_sums[0], 1)
    received = [
        stepped(value, 2 * i + 3, 2 * i + 2) for i, value in enumerate(near_sums[1:])
    ]
    own_sum, other_sum = pl.pallas_call(
        split_kernel,
        out_shape=[jax.ShapeDtypeStruct(block_shape, jnp.float32)] * 2,
        in_specs=[VMEM_SPEC] * (1 + chip_messages),
        out_specs=[VMEM_SPEC] * 2,
        compiler_params=params,
        cost_estimate=cost(6.0),
        name="split_sums",
    )(own_sum, *received)
    other_sum = flipped(other_sum, 1)
    second = stacked("mine_2", 3.0, near_sums[0], *pairs[2:3])
    others = stacked("mine_3", 3.0, second, *pairs[3:])
    mine = stacked("mine", 0.1, others, pair, pairs[1], second, others)
    other = flipped(mine, 1)

    own_grads, dots = pl.pallas_call(
        functools.partial(owner_sum_kernel, norm),
        out_shape=(
            jax.ShapeDtypeStruct((1,) + block_shape, jnp.float32),
            jax.ShapeDtypeStruct((cap, side), jnp.float32),
        ),
        in_specs=[VMEM_SPEC] * 5,
        out_specs=(VMEM_SPEC, VMEM_SPEC),
        compiler_params=params,
        cost_estimate=cost(6.0),
        name="owner_sums",
    )(scale_rows, stored, own_sum, other_sum, neighbour)
    other_dots = lax.ppermute(dots, "group", [(0, 1), (1, 0)])
    grad_inputs_t, block_grads = pl.pallas_call(
        input_grad_kernel,
        out_shape=(
            jax.ShapeDtypeStruct(inputs_t.shape, jnp.bfloat16),
            jax.ShapeDtypeStruct((1,) + block_shape, jnp.float32),
        ),
        in_specs=[SMEM_SPEC] + [VMEM_SPEC] * 4,
        out_specs=(VMEM_SPEC, VMEM_SPEC),
        scratch_shapes=[pltpu.VMEM(inputs_t.shape, jnp.float32)],
        compiler_params=params,
        cost_estimate=cost(2.0),
        name="input_grads",
    )(table, columns, mine, other, own_grads)
    scale_grads = pl.pallas_call(
        finish_kernel,
        out_shape=jax.ShapeDtypeStruct((1, cap), jnp.float32),
        in_specs=[VMEM_SPEC] * 2 + [HBM_SPEC],
        out_specs=VMEM_SPEC,
        compiler_params=params,
        cost_estimate=cost(0.5),
        name="finish",
    )(dots, other_dots, in_hbm(grad_inputs_t))
    return (grad_inputs_t, block_grads, scale_grads)


def solution(mesh):
    return jax.shard_map(
        on_device,
        mesh=mesh,
        in_specs=(
            P(None, "group", "dp"),
            P(None, None, None, "dp"),
            P("dp", None, "group", None),
            P("dp", None),
            P(),
            P(),
            P(),
        ),
        out_specs=(P(None, "group", "dp"), P("dp", None, "group", None), P("dp", None)),
        check_vma=False,
    )
```

```python
import functools
import math

import jax
import jax.numpy as jnp
from jax import lax
from jax.experimental import pallas as pl
from jax.experimental.pallas import tpu as pltpu
from jax.sharding import PartitionSpec as P

VMEM_LIMIT = 48 * 1024 * 1024
TAIL = 16
UNIT = 2.0**15
SMEM_SPEC = pl.BlockSpec(memory_space=pltpu.SMEM)
VMEM_SPEC = pl.BlockSpec(memory_space=pltpu.VMEM)
ANY_SPEC = pl.BlockSpec(memory_space=pl.ANY)
HBM_SPEC = pl.BlockSpec(memory_space=pltpu.HBM)


def magic_divide(value, divisor, limit):
    shift = 20
    factor = -(-(1 << shift) // divisor)
    assert limit * factor < 1 << 31
    assert all((v * factor) >> shift == v // divisor for v in range(limit))
    return (value * factor) >> shift


def partial_kernel(
    kept_hbm, assign_hbm, counts_hbm, x_hbm, grad_ref, stored_hbm, scales_hbm,
    near_keep, near_send, far_keep, far_send, cols_ref, tab_ref, scaled_ref, stored_ref, scale_rows,
    part_ref, x_ref, scales_ref, kept, assign, counts, slot_ref, sem, index_sems, x_sem
):
    x_copy = pltpu.make_async_copy(x_hbm, x_ref, x_sem)
    index_copies = [
        pltpu.make_async_copy(source, target, index_sems.at[i])
        for i, (source, target) in enumerate(
            (
                (assign_hbm, assign),
                (kept_hbm, kept),
                (counts_hbm, counts),
                (scales_hbm, scales_ref),
                (stored_hbm, stored_ref),
            )
        )
    ]
    for copy in index_copies:
        copy.start()
    x_copy.start()
    keep_count = kept.shape[1]
    hid_blocks = grad_ref.shape[1]
    total = x_ref.shape[0] * hid_blocks
    owners = counts.shape[0]
    entries = assign.shape[0]
    outer, cap = near_keep.shape[:2]
    me = lax.axis_index("dp")
    part_ref[...] = jnp.zeros_like(part_ref)
    for copy in index_copies[:2]:
        copy.wait()

    def fetch_step(p, carry):
        entry = assign[p]
        matrix = jnp.where(entry >= keep_count, 1, 0)
        block = kept[matrix, entry - matrix * keep_count]
        row = magic_divide(block, hid_blocks, total)
        column = block - row * hid_blocks
        pltpu.make_async_copy(grad_ref.at[matrix, column], cols_ref.at[p], sem).start()
        tab_ref[0, p] = row
        return carry

    lax.fori_loop(0, entries, fetch_step, 0, unroll=min(entries, 24))
    for copy in index_copies[2:]:
        copy.wait()

    def owner_step(owner, offset):
        kind = (owner & 3) ^ (me & 3)
        if is_paired(outer):
            step_to = step_from = (owner >> 2) ^ (me >> 2)
        else:
            away = (owner >> 2) - (me >> 2)
            step_to = jnp.where(away < 0, away + outer, away)
            step_from = jnp.where(away > 0, outer - away, -away)
        split = step_to >= 2
        summing = jnp.where(split, 1 - (step_to & 1), owner & 1)
        place = jnp.where(split, (step_to & ~1) + (owner & 1), step_to)
        part = (kind & 2) | (summing ^ (me & 1))
        for c in range(cap):

            @pl.when(c < counts[owner])
            def _():
                p = offset + c
                slot_ref[p] = (part * outer + place) * cap + c
                tab_ref[1, p] = kind
                tab_ref[2, p] = step_from
                tab_ref[3, p] = c

        return offset + counts[owner]

    lax.fori_loop(0, owners, owner_step, 0, unroll=min(owners, 16))
    for c in range(cap):
        scaled = scales_ref[0, c] * stored_ref[0, c].astype(jnp.float32)
        scaled_ref[c] = scaled.astype(jnp.bfloat16)
        scale_rows[c] = jnp.full(scale_rows.shape[1:], scales_ref[0, c], jnp.float32)
    x_copy.wait()
    pltpu.make_async_copy(cols_ref, cols_ref, sem).wait()

    def entry_step(p, carry):
        part_ref[slot_ref[p]] = lax.dot_general(
            x_ref[tab_ref[0, p]],
            cols_ref[p],
            (((1,), (1,)), ((), ())),
            preferred_element_type=jnp.float32,
        )
        return carry

    lax.fori_loop(0, entries, entry_step, 0, unroll=min(entries, 24))
    size = outer * cap
    for kind, ref in enumerate((near_keep, near_send, far_keep, far_send)):
        ref[...] = part_ref[kind * size : (kind + 1) * size].reshape(ref.shape)


def encode(total):
    largest = jnp.max(jnp.abs(total), axis=0, keepdims=True)
    power = jnp.ceil(jnp.log2(jnp.maximum(largest, 2.0**-126)))
    power = jnp.clip(power, -126.0, 126.0)
    level = jnp.floor(total * jnp.exp2(-power) * UNIT + 0.5)
    level = jnp.clip(level, -UNIT, UNIT - 1.0)
    return level.astype(jnp.int32).astype(jnp.int16), power


def message_rows(blocks, slab_rows):
    return blocks * slab_rows + -(-blocks // TAIL) * TAIL


def write_message(totals, out_ref):
    blocks, (slab_rows, side) = len(totals), totals[0].shape
    tail_rows = out_ref.shape[0] - blocks * slab_rows
    tail_row = lax.broadcasted_iota(jnp.int32, (tail_rows, side), 0)
    tail = jnp.zeros((tail_rows, side), jnp.float32)
    for i, total in enumerate(totals):
        level, power = encode(total)
        out_ref[i * slab_rows : (i + 1) * slab_rows] = level
        tail = jnp.where(tail_row == i, power, tail)
    out_ref[blocks * slab_rows :] = tail.astype(jnp.int32).astype(jnp.int16)


def read_message(blocks, slab_rows, ref):
    powers = ref[blocks * slab_rows :].astype(jnp.int32).astype(jnp.float32)
    units = jnp.exp2(powers) * (1.0 / UNIT)
    totals = []
    for i in range(blocks):
        level = ref[i * slab_rows : (i + 1) * slab_rows].astype(jnp.int32)
        totals.append(level.astype(jnp.float32) * units[i : i + 1])
    return totals


def far_sum_kernel(keep_ref, got_ref, near_send, out_ref, near_out):
    near_out[...] = near_send[...]
    outer, cap = keep_ref.shape[:2]
    totals = [keep_ref[k, c] + got_ref[k, c] for k in range(outer) for c in range(cap)]
    write_message(totals, out_ref)


def near_sum_kernel(keep_ref, got_ref, far_ref, own_ref, *out_refs):
    outer, cap, slab_rows, side = keep_ref.shape
    far = read_message(outer * cap, slab_rows, far_ref)

    def totals(places):
        return [keep_ref[k, c] + got_ref[k, c] + far[k * cap + c] for k in places for c in range(cap)]

    for c, total in enumerate(totals([0])):
        own_ref[c] = total
    write_message(totals([1]), out_refs[0])
    for i, out_ref in enumerate(out_refs[1:]):
        write_message(totals([2 * i + 2, 2 * i + 3]), out_ref)


def split_kernel(own_ref, neighbour_ref, *refs):
    *got_refs, mine_ref, other_ref = refs
    cap, slab_rows, side = own_ref.shape
    first_core = (lax.axis_index("dp") & 1) == 0
    neighbour = read_message(cap, slab_rows, neighbour_ref)
    sums = [[own_ref[c] + neighbour[c] for c in range(cap)], [jnp.zeros((slab_rows, side), jnp.float32)] * cap]
    for got_ref in got_refs:
        blocks = read_message(2 * cap, slab_rows, got_ref)
        for c in range(cap):
            sums[0][c] = sums[0][c] + jnp.where(first_core, blocks[c], blocks[cap + c])
            sums[1][c] = sums[1][c] + jnp.where(first_core, blocks[cap + c], blocks[c])
    for c in range(cap):
        mine_ref[c] = sums[0][c]
        other_ref[c] = sums[1][c]


def stack_kernel(count, *refs):
    in_refs, out_ref = refs[:count], refs[-1]
    at = 0
    for in_ref in in_refs:
        if in_ref.ndim < out_ref.ndim:
            out_ref[at] = in_ref[...]
            at += 1
        else:
            out_ref[at : at + in_ref.shape[0]] = in_ref[...]
            at += in_ref.shape[0]


def input_grad_kernel(tab_ref, cols_ref, mine, other, block_ref, out_ref, block_out, acc_ref):
    entries = cols_ref.shape[0]
    block_out[...] = block_ref[...]
    acc_ref[...] = jnp.zeros_like(acc_ref)

    def entry_step(p, carry):
        kind, behind, c = tab_ref[1, p], tab_ref[2, p], tab_ref[3, p]
        block = jnp.where(
            (kind & 1) == 0, mine[behind, kind >> 1, c], other[behind, kind >> 1, c]
        )
        row = tab_ref[0, p]
        acc_ref[row] += jnp.dot(block, cols_ref[p], preferred_element_type=jnp.float32)
        return carry

    lax.fori_loop(0, entries, entry_step, 0, unroll=min(entries, 24))
    out_ref[...] = acc_ref[...].astype(out_ref.dtype)


def owner_sum_kernel(norm, scales_ref, stored_ref, own_ref, other_ref, block_ref, dots_ref):
    cap, slab_rows, side = stored_ref.shape[1:]
    totals = [own_ref[c] + other_ref[c] for c in range(cap)]
    for c in range(cap):
        gradient = totals[c] * norm
        block_ref[0, c] = scales_ref[c, 0:1] * gradient
        dots_ref[c : c + 1, :] = jnp.sum(
            stored_ref[0, c].astype(jnp.float32) * gradient, axis=0, keepdims=True
        )


def finish_kernel(dots_ref, got_ref, grads_ref, scale_out):
    del grads_ref
    total = jnp.sum(dots_ref[...] + got_ref[...], axis=1, keepdims=True)
    cap = total.shape[0]
    row = lax.broadcasted_iota(jnp.int32, (cap, cap), 0)
    column = lax.broadcasted_iota(jnp.int32, (cap, cap), 1)
    scale_out[...] = jnp.sum(jnp.where(row == column, total, 0.0), axis=0, keepdims=True)


def cost(microseconds):
    return pl.CostEstimate(
        flops=int(microseconds * 1_153_000_000), bytes_accessed=int(microseconds * 3_690_000), transcendentals=0
    )


def in_hbm(value):
    return pltpu.with_memory_space_constraint(value, pltpu.HBM)


def flipped(value, bit):
    return lax.ppermute(value, "dp", [(i, i ^ bit) for i in range(lax.axis_size("dp"))])


def is_paired(size):
    return size & (size - 1) == 0


def ahead(places, start, step):
    return start ^ step if is_paired(places) else (start + step) % places


def stepped(value, step, second_core_step=None):
    size = lax.axis_size("dp")
    steps = (step, step if second_core_step is None else second_core_step)
    return lax.ppermute(
        value,
        "dp",
        [(i, ahead(size // 4, i // 4, steps[i % 2]) * 4 + i % 4) for i in range(size)],
    )


def stacked(name, estimate, after, *values):
    single = min(value.ndim for value in values)
    count = sum(1 if value.ndim == single else value.shape[0] for value in values)
    shape = (count,) + values[0].shape
    return pl.pallas_call(
        functools.partial(stack_kernel, len(values)),
        out_shape=jax.ShapeDtypeStruct(shape, values[0].dtype),
        in_specs=[VMEM_SPEC] * len(values) + [ANY_SPEC] * len(after),
        out_specs=VMEM_SPEC,
        compiler_params=pltpu.CompilerParams(vmem_limit_bytes=VMEM_LIMIT),
        cost_estimate=cost(estimate),
        name=name,
    )(*values, *after)


def on_device(
    inputs_t, grad_proj, stored_blocks, block_scales, kept_blocks, assignment, owner_counts
):
    row_blocks, slab_rows, tokens_here = inputs_t.shape
    cap, side = stored_blocks.shape[1], stored_blocks.shape[3]
    entries = assignment.shape[0]
    devices = lax.axis_size("dp")
    outer = devices // 4
    norm = 1.0 / math.sqrt(tokens_here * devices)
    params = pltpu.CompilerParams(vmem_limit_bytes=VMEM_LIMIT)
    block_shape = (cap, slab_rows, side)
    side_shape = (outer, cap, slab_rows, side)
    message_shape = (message_rows(cap, slab_rows), side)

    near_keep, near_send, far_keep, far_send, columns, table, scaled, stored, scale_rows = pl.pallas_call(
        partial_kernel,
        out_shape=[jax.ShapeDtypeStruct(side_shape, jnp.float32)] * 4
        + [
            jax.ShapeDtypeStruct((entries, side, tokens_here), jnp.bfloat16),
            jax.ShapeDtypeStruct((4, entries), jnp.int32),
            jax.ShapeDtypeStruct(block_shape, jnp.bfloat16),
            jax.ShapeDtypeStruct(stored_blocks.shape, jnp.bfloat16),
            jax.ShapeDtypeStruct((cap, 8, side), jnp.float32),
        ],
        in_specs=[HBM_SPEC] * 7,
        out_specs=[VMEM_SPEC] * 5 + [SMEM_SPEC] + [VMEM_SPEC] * 3,
        scratch_shapes=[
            pltpu.VMEM((4 * outer * cap, slab_rows, side), jnp.float32),
            pltpu.VMEM(inputs_t.shape, inputs_t.dtype),
            pltpu.SMEM(block_scales.shape, jnp.float32),
            pltpu.SMEM(kept_blocks.shape, jnp.int32),
            pltpu.SMEM(assignment.shape, jnp.int32),
            pltpu.SMEM(owner_counts.shape, jnp.int32),
            pltpu.SMEM((entries,), jnp.int32),
            pltpu.SemaphoreType.DMA,
            pltpu.SemaphoreType.DMA((5,)),
            pltpu.SemaphoreType.DMA,
        ],
        compiler_params=params,
        cost_estimate=cost(3.5),
        name="partials",
    )(
        *map(
            in_hbm,
            (
                kept_blocks,
                assignment,
                owner_counts,
                inputs_t,
                grad_proj,
                stored_blocks,
                block_scales,
            ),
        )
    )

    far_got = flipped(far_send, 1)
    far_scaled = flipped(scaled, 2)
    far_sums, near_send = pl.pallas_call(
        far_sum_kernel,
        out_shape=(
            jax.ShapeDtypeStruct((message_rows(outer * cap, slab_rows), side), jnp.int16),
            jax.ShapeDtypeStruct(side_shape, jnp.float32),
        ),
        in_specs=[VMEM_SPEC] * 3,
        out_specs=(VMEM_SPEC, VMEM_SPEC),
        compiler_params=params,
        cost_estimate=cost(3.0),
        name="far_sums",
    )(far_keep, far_got, near_send)
    near_got = flipped(near_send, 1)

    pair = stacked("pair", 5.0, (far_sums,), scaled, far_scaled)
    forwarded = [s for s in range(1, outer) if is_paired(outer) and s & (s - 1)]
    pairs = {0: pair}
    for step in range(1, outer):
        if step not in forwarded:
            pairs[step] = stepped(pair, step)
    message = jax.ShapeDtypeStruct(message_shape, jnp.int16)
    chip_message = jax.ShapeDtypeStruct((message_rows(2 * cap, slab_rows), side), jnp.int16)
    chip_messages = outer // 2 - 1
    own_sum, *near_sums = pl.pallas_call(
        near_sum_kernel,
        out_shape=[jax.ShapeDtypeStruct(block_shape, jnp.float32), message]
        + [chip_message] * chip_messages,
        in_specs=[VMEM_SPEC] * 3,
        out_specs=[VMEM_SPEC] * (2 + chip_messages),
        compiler_params=params,
        cost_estimate=cost(0.3),
        name="near_sums",
    )(near_keep, near_got, flipped(far_sums, 2))
    neighbour = stepped(near_sums[0], 1)
    received = [
        stepped(value, 2 * i + 3, 2 * i + 2) for i, value in enumerate(near_sums[1:])
    ]
    own_sum, other_sum = pl.pallas_call(
        split_kernel,
        out_shape=[jax.ShapeDtypeStruct(block_shape, jnp.float32)] * 2,
        in_specs=[VMEM_SPEC] * (2 + chip_messages),
        out_specs=[VMEM_SPEC] * 2,
        compiler_params=params,
        cost_estimate=cost(6.0),
        name="split_sums",
    )(own_sum, neighbour, *received)
    other_sum = flipped(other_sum, 1)
    for step in forwarded:
        near_bit = step & -step
        after = (near_sums[0], pairs[near_bit])
        held = stacked("hold_%d" % step, 0.1, after, pairs[step ^ near_bit])[0]
        pairs[step] = stepped(held, near_bit)
    mine = stacked("mine", 0.1, near_sums[:1], *(pairs[step] for step in range(outer)))
    other = flipped(mine, 1)

    own_grads, dots = pl.pallas_call(
        functools.partial(owner_sum_kernel, norm),
        out_shape=(
            jax.ShapeDtypeStruct((1,) + block_shape, jnp.float32),
            jax.ShapeDtypeStruct((cap, side), jnp.float32),
        ),
        in_specs=[VMEM_SPEC] * 4,
        out_specs=(VMEM_SPEC, VMEM_SPEC),
        compiler_params=params,
        cost_estimate=cost(6.0),
        name="owner_sums",
    )(scale_rows, stored, own_sum, other_sum)
    other_dots = lax.ppermute(dots, "group", [(0, 1), (1, 0)])
    grad_inputs_t, block_grads = pl.pallas_call(
        input_grad_kernel,
        out_shape=(
            jax.ShapeDtypeStruct(inputs_t.shape, jnp.bfloat16),
            jax.ShapeDtypeStruct((1,) + block_shape, jnp.float32),
        ),
        in_specs=[SMEM_SPEC] + [VMEM_SPEC] * 4,
        out_specs=(VMEM_SPEC, VMEM_SPEC),
        scratch_shapes=[pltpu.VMEM(inputs_t.shape, jnp.float32)],
        compiler_params=params,
        cost_estimate=cost(2.0),
        name="input_grads",
    )(table, columns, mine, other, own_grads)
    scale_grads = pl.pallas_call(
        finish_kernel,
        out_shape=jax.ShapeDtypeStruct((1, cap), jnp.float32),
        in_specs=[VMEM_SPEC] * 2 + [HBM_SPEC],
        out_specs=VMEM_SPEC,
        compiler_params=params,
        cost_estimate=cost(0.5),
        name="finish",
    )(dots, other_dots, in_hbm(grad_inputs_t))
    return (grad_inputs_t, block_grads, scale_grads)


def solution(mesh):
    return jax.shard_map(
        on_device,
        mesh=mesh,
        in_specs=(
            P(None, "group", "dp"),
            P(None, None, None, "dp"),
            P("dp", None, "group", None),
            P("dp", None),
            P(),
            P(),
            P(),
        ),
        out_specs=(P(None, "group", "dp"), P("dp", None, "group", None), P("dp", None)),
        check_vma=False,
    )
```

```python
import functools
import math

import jax
import jax.numpy as jnp
from jax import lax
from jax.experimental import pallas as pl
from jax.experimental.pallas import tpu as pltpu
from jax.sharding import PartitionSpec as P

VMEM_LIMIT = 48 * 1024 * 1024
TAIL = 16
UNIT = 2.0**15
SMEM_SPEC = pl.BlockSpec(memory_space=pltpu.SMEM)
VMEM_SPEC = pl.BlockSpec(memory_space=pltpu.VMEM)
ANY_SPEC = pl.BlockSpec(memory_space=pl.ANY)
HBM_SPEC = pl.BlockSpec(memory_space=pltpu.HBM)


def magic_divide(value, divisor, limit):
    shift = 20
    factor = -(-(1 << shift) // divisor)
    assert limit * factor < 1 << 31
    assert all((v * factor) >> shift == v // divisor for v in range(limit))
    return (value * factor) >> shift


def partial_kernel(
    kept_hbm, assign_hbm, counts_hbm, x_hbm, grad_ref, stored_hbm, scales_hbm,
    near_keep, near_send, far_keep, far_send, cols_ref, tab_ref, scaled_ref, stored_ref, scale_rows,
    part_ref, x_ref, scales_ref, kept, assign, counts, slot_ref, sem, index_sems, x_sem
):
    x_copy = pltpu.make_async_copy(x_hbm, x_ref, x_sem)
    pieces = 4 if kept.shape[1] % 512 == 0 else 1
    width = kept.shape[1] // pieces
    columns = [pl.ds(i * width, width) for i in range(pieces)]
    early = [(assign_hbm, assign)] + [(kept_hbm.at[:, c], kept.at[:, c]) for c in columns]
    late = [(counts_hbm, counts), (scales_hbm, scales_ref), (stored_hbm, stored_ref)]
    index_copies = [
        pltpu.make_async_copy(source, target, index_sems.at[i])
        for i, (source, target) in enumerate(early + late)
    ]
    for copy in index_copies:
        copy.start()
    x_copy.start()
    keep_count = kept.shape[1]
    hid_blocks = grad_ref.shape[1]
    total = x_ref.shape[0] * hid_blocks
    owners = counts.shape[0]
    entries = assign.shape[0]
    outer, cap = near_keep.shape[:2]
    me = lax.axis_index("dp")
    part_ref[...] = jnp.zeros_like(part_ref)
    for copy in index_copies[: len(early)]:
        copy.wait()

    def fetch_step(p, carry):
        entry = assign[p]
        matrix = jnp.where(entry >= keep_count, 1, 0)
        block = kept[matrix, entry - matrix * keep_count]
        row = magic_divide(block, hid_blocks, total)
        column = block - row * hid_blocks
        pltpu.make_async_copy(grad_ref.at[matrix, column], cols_ref.at[p], sem).start()
        tab_ref[0, p] = row
        return carry

    lax.fori_loop(0, entries, fetch_step, 0, unroll=min(entries, 24))
    for copy in index_copies[len(early) :]:
        copy.wait()

    def owner_step(owner, offset):
        kind = (owner & 3) ^ (me & 3)
        if is_paired(outer):
            step_to = step_from = (owner >> 2) ^ (me >> 2)
        else:
            away = (owner >> 2) - (me >> 2)
            step_to = jnp.where(away < 0, away + outer, away)
            step_from = jnp.where(away > 0, outer - away, -away)
        for c in range(cap):

            @pl.when(c < counts[owner])
            def _():
                p = offset + c
                slot_ref[p] = (kind * outer + step_to) * cap + c
                tab_ref[1, p] = kind
                tab_ref[2, p] = step_from
                tab_ref[3, p] = c

        return offset + counts[owner]

    lax.fori_loop(0, owners, owner_step, 0, unroll=min(owners, 16))
    for c in range(cap):
        scaled = scales_ref[0, c] * stored_ref[0, c].astype(jnp.float32)
        scaled_ref[c] = scaled.astype(jnp.bfloat16)
        scale_rows[c] = jnp.full(scale_rows.shape[1:], scales_ref[0, c], jnp.float32)
    x_copy.wait()
    pltpu.make_async_copy(cols_ref, cols_ref, sem).wait()

    def entry_step(p, carry):
        part_ref[slot_ref[p]] = lax.dot_general(
            x_ref[tab_ref[0, p]],
            cols_ref[p],
            (((1,), (1,)), ((), ())),
            preferred_element_type=jnp.float32,
        )
        return carry

    lax.fori_loop(0, entries, entry_step, 0, unroll=min(entries, 24))
    size = outer * cap
    for kind, ref in enumerate((near_keep, near_send, far_keep, far_send)):
        ref[...] = part_ref[kind * size : (kind + 1) * size].reshape(ref.shape)


def encode(total):
    largest = jnp.max(jnp.abs(total), axis=0, keepdims=True)
    power = jnp.ceil(jnp.log2(jnp.maximum(largest, 2.0**-126)))
    power = jnp.clip(power, -126.0, 126.0)
    level = jnp.floor(total * jnp.exp2(-power) * UNIT + 0.5)
    level = jnp.clip(level, -UNIT, UNIT - 1.0)
    return level.astype(jnp.int32).astype(jnp.int16), power


def message_rows(blocks, slab_rows):
    return blocks * slab_rows + -(-blocks // TAIL) * TAIL


def write_message(totals, out_ref):
    blocks, (slab_rows, side) = len(totals), totals[0].shape
    tail_rows = out_ref.shape[0] - blocks * slab_rows
    tail_row = lax.broadcasted_iota(jnp.int32, (tail_rows, side), 0)
    tail = jnp.zeros((tail_rows, side), jnp.float32)
    for i, total in enumerate(totals):
        level, power = encode(total)
        out_ref[i * slab_rows : (i + 1) * slab_rows] = level
        tail = jnp.where(tail_row == i, power, tail)
    out_ref[blocks * slab_rows :] = tail.astype(jnp.int32).astype(jnp.int16)


def read_message(blocks, slab_rows, ref):
    powers = ref[blocks * slab_rows :].astype(jnp.int32).astype(jnp.float32)
    units = jnp.exp2(powers) * (1.0 / UNIT)
    totals = []
    for i in range(blocks):
        level = ref[i * slab_rows : (i + 1) * slab_rows].astype(jnp.int32)
        totals.append(level.astype(jnp.float32) * units[i : i + 1])
    return totals


def far_sum_kernel(keep_ref, got_ref, near_send, out_ref, near_out):
    near_out[...] = near_send[...]
    outer, cap = keep_ref.shape[:2]
    totals = [keep_ref[k, c] + got_ref[k, c] for k in range(outer) for c in range(cap)]
    write_message(totals, out_ref)


def near_sum_kernel(keep_ref, got_ref, far_ref, *out_refs):
    outer, cap, slab_rows, side = keep_ref.shape
    far = read_message(outer * cap, slab_rows, far_ref)
    for step in range(outer):
        totals = [
            keep_ref[step, c] + got_ref[step, c] + far[step * cap + c] for c in range(cap)
        ]
        if step == 0:
            for c in range(cap):
                out_refs[0][c] = totals[c]
        else:
            write_message(totals, out_refs[step])


def add_kernel(own_ref, *refs):
    *got_refs, out_ref = refs
    cap, slab_rows, side = own_ref.shape
    totals = [own_ref[c] for c in range(cap)]
    for got_ref in got_refs:
        totals = [a + b for a, b in zip(totals, read_message(cap, slab_rows, got_ref))]
    for c in range(cap):
        out_ref[c] = totals[c]


def stack_kernel(*refs):
    *in_refs, _, out_ref = refs
    at = 0
    for in_ref in in_refs:
        if in_ref.ndim < out_ref.ndim:
            out_ref[at] = in_ref[...]
            at += 1
        else:
            out_ref[at : at + in_ref.shape[0]] = in_ref[...]
            at += in_ref.shape[0]


def input_grad_kernel(tab_ref, cols_ref, mine, other, block_ref, out_ref, block_out, acc_ref):
    entries = cols_ref.shape[0]
    block_out[...] = block_ref[...]
    acc_ref[...] = jnp.zeros_like(acc_ref)

    def entry_step(p, carry):
        kind, behind, c = tab_ref[1, p], tab_ref[2, p], tab_ref[3, p]
        block = jnp.where(
            (kind & 1) == 0, mine[behind, kind >> 1, c], other[behind, kind >> 1, c]
        )
        row = tab_ref[0, p]
        acc_ref[row] += jnp.dot(block, cols_ref[p], preferred_element_type=jnp.float32)
        return carry

    lax.fori_loop(0, entries, entry_step, 0, unroll=min(entries, 24))
    out_ref[...] = acc_ref[...].astype(out_ref.dtype)


def owner_sum_kernel(norm, scales_ref, stored_ref, own_ref, *refs):
    got_refs, (block_ref, dots_ref) = refs[:-2], refs[-2:]
    cap, slab_rows, side = stored_ref.shape[1:]
    totals = [own_ref[c] for c in range(cap)]
    for got_ref in got_refs:
        totals = [a + b for a, b in zip(totals, read_message(cap, slab_rows, got_ref))]
    for c in range(cap):
        gradient = totals[c] * norm
        block_ref[0, c] = scales_ref[c, 0:1] * gradient
        dots_ref[c : c + 1, :] = jnp.sum(
            stored_ref[0, c].astype(jnp.float32) * gradient, axis=0, keepdims=True
        )


def finish_kernel(dots_ref, got_ref, grads_ref, scale_out):
    del grads_ref
    total = jnp.sum(dots_ref[...] + got_ref[...], axis=1, keepdims=True)
    cap = total.shape[0]
    row = lax.broadcasted_iota(jnp.int32, (cap, cap), 0)
    column = lax.broadcasted_iota(jnp.int32, (cap, cap), 1)
    scale_out[...] = jnp.sum(jnp.where(row == column, total, 0.0), axis=0, keepdims=True)


def cost(microseconds):
    return pl.CostEstimate(
        flops=int(microseconds * 1_153_000_000), bytes_accessed=int(microseconds * 3_690_000), transcendentals=0
    )


def in_hbm(value):
    return pltpu.with_memory_space_constraint(value, pltpu.HBM)


def flipped(value, bit):
    return lax.ppermute(value, "dp", [(i, i ^ bit) for i in range(lax.axis_size("dp"))])


def is_paired(size):
    return size & (size - 1) == 0


def ahead(places, start, step):
    return start ^ step if is_paired(places) else (start + step) % places


def stepped(value, step):
    size = lax.axis_size("dp")
    return lax.ppermute(
        value, "dp", [(i, ahead(size // 4, i // 4, step) * 4 + i % 4) for i in range(size)]
    )


def stacked(name, estimate, after, *values):
    single = min(value.ndim for value in values)
    count = sum(1 if value.ndim == single else value.shape[0] for value in values)
    shape = (count,) + values[0].shape
    return pl.pallas_call(
        stack_kernel,
        out_shape=jax.ShapeDtypeStruct(shape, values[0].dtype),
        in_specs=[VMEM_SPEC] * len(values) + [ANY_SPEC],
        out_specs=VMEM_SPEC,
        compiler_params=pltpu.CompilerParams(vmem_limit_bytes=VMEM_LIMIT),
        cost_estimate=cost(estimate),
        name=name,
    )(*values, after)


def on_device(
    inputs_t, grad_proj, stored_blocks, block_scales, kept_blocks, assignment, owner_counts
):
    row_blocks, slab_rows, tokens_here = inputs_t.shape
    cap, side = stored_blocks.shape[1], stored_blocks.shape[3]
    entries = assignment.shape[0]
    devices = lax.axis_size("dp")
    outer = devices // 4
    norm = 1.0 / math.sqrt(tokens_here * devices)
    params = pltpu.CompilerParams(vmem_limit_bytes=VMEM_LIMIT)
    block_shape = (cap, slab_rows, side)
    side_shape = (outer, cap, slab_rows, side)
    message_shape = (message_rows(cap, slab_rows), side)

    near_keep, near_send, far_keep, far_send, columns, table, scaled, stored, scale_rows = pl.pallas_call(
        partial_kernel,
        out_shape=[jax.ShapeDtypeStruct(side_shape, jnp.float32)] * 4
        + [
            jax.ShapeDtypeStruct((entries, side, tokens_here), jnp.bfloat16),
            jax.ShapeDtypeStruct((4, entries), jnp.int32),
            jax.ShapeDtypeStruct(block_shape, jnp.bfloat16),
            jax.ShapeDtypeStruct(stored_blocks.shape, jnp.bfloat16),
            jax.ShapeDtypeStruct((cap, 8, side), jnp.float32),
        ],
        in_specs=[HBM_SPEC] * 7,
        out_specs=[VMEM_SPEC] * 5 + [SMEM_SPEC] + [VMEM_SPEC] * 3,
        scratch_shapes=[
            pltpu.VMEM((4 * outer * cap, slab_rows, side), jnp.float32),
            pltpu.VMEM(inputs_t.shape, inputs_t.dtype),
            pltpu.SMEM(block_scales.shape, jnp.float32),
            pltpu.SMEM(kept_blocks.shape, jnp.int32),
            pltpu.SMEM(assignment.shape, jnp.int32),
            pltpu.SMEM(owner_counts.shape, jnp.int32),
            pltpu.SMEM((entries,), jnp.int32),
            pltpu.SemaphoreType.DMA,
            pltpu.SemaphoreType.DMA((8,)),
            pltpu.SemaphoreType.DMA,
        ],
        compiler_params=params,
        cost_estimate=cost(3.5),
        name="partials",
    )(
        *map(
            in_hbm,
            (
                kept_blocks,
                assignment,
                owner_counts,
                inputs_t,
                grad_proj,
                stored_blocks,
                block_scales,
            ),
        )
    )

    far_got = flipped(far_send, 1)
    far_scaled = flipped(scaled, 2)
    far_sums, near_send = pl.pallas_call(
        far_sum_kernel,
        out_shape=(
            jax.ShapeDtypeStruct((message_rows(outer * cap, slab_rows), side), jnp.int16),
            jax.ShapeDtypeStruct(side_shape, jnp.float32),
        ),
        in_specs=[VMEM_SPEC] * 3,
        out_specs=(VMEM_SPEC, VMEM_SPEC),
        compiler_params=params,
        cost_estimate=cost(3.0),
        name="far_sums",
    )(far_keep, far_got, near_send)
    near_got = flipped(near_send, 1)

    pair = stacked("pair", 5.0, far_sums, scaled, far_scaled)
    pairs = [pair] + [stepped(pair, step) for step in range(1, outer)]
    own_sum, *near_sums = pl.pallas_call(
        near_sum_kernel,
        out_shape=[jax.ShapeDtypeStruct(block_shape, jnp.float32)]
        + [jax.ShapeDtypeStruct(message_shape, jnp.int16)] * (outer - 1),
        in_specs=[VMEM_SPEC] * 3,
        out_specs=[VMEM_SPEC] * outer,
        compiler_params=params,
        cost_estimate=cost(0.3),
        name="near_sums",
    )(near_keep, near_got, flipped(far_sums, 2))
    received = [stepped(value, step + 1) for step, value in enumerate(near_sums)]

    for number, group in enumerate((received[2:], received[1:2])):
        own_sum = pl.pallas_call(
            add_kernel,
            out_shape=jax.ShapeDtypeStruct(block_shape, jnp.float32),
            in_specs=[VMEM_SPEC] * (1 + len(group)),
            out_specs=VMEM_SPEC,
            compiler_params=params,
            cost_estimate=cost(6.0),
            name="add_%d" % number,
        )(own_sum, *group)
    second = stacked("mine_2", 3.0, near_sums[0], *pairs[2:3])
    others = stacked("mine_3", 3.0, second, *pairs[3:])
    mine = stacked("mine", 0.1, others, pair, pairs[1], second, others)
    other = flipped(mine, 1)

    own_grads, dots = pl.pallas_call(
        functools.partial(owner_sum_kernel, norm),
        out_shape=(
            jax.ShapeDtypeStruct((1,) + block_shape, jnp.float32),
            jax.ShapeDtypeStruct((cap, side), jnp.float32),
        ),
        in_specs=[VMEM_SPEC] * 4,
        out_specs=(VMEM_SPEC, VMEM_SPEC),
        compiler_params=params,
        cost_estimate=cost(6.0),
        name="owner_sums",
    )(scale_rows, stored, own_sum, received[0])
    other_dots = lax.ppermute(dots, "group", [(0, 1), (1, 0)])
    grad_inputs_t, block_grads = pl.pallas_call(
        input_grad_kernel,
        out_shape=(
            jax.ShapeDtypeStruct(inputs_t.shape, jnp.bfloat16),
            jax.ShapeDtypeStruct((1,) + block_shape, jnp.float32),
        ),
        in_specs=[SMEM_SPEC] + [VMEM_SPEC] * 4,
        out_specs=(VMEM_SPEC, VMEM_SPEC),
        scratch_shapes=[pltpu.VMEM(inputs_t.shape, jnp.float32)],
        compiler_params=params,
        cost_estimate=cost(2.0),
        name="input_grads",
    )(table, columns, mine, other, own_grads)
    scale_grads = pl.pallas_call(
        finish_kernel,
        out_shape=jax.ShapeDtypeStruct((1, cap), jnp.float32),
        in_specs=[VMEM_SPEC] * 2 + [HBM_SPEC],
        out_specs=VMEM_SPEC,
        compiler_params=params,
        cost_estimate=cost(0.5),
        name="finish",
    )(dots, other_dots, in_hbm(grad_inputs_t))
    return (grad_inputs_t, block_grads, scale_grads)


def solution(mesh):
    return jax.shard_map(
        on_device,
        mesh=mesh,
        in_specs=(
            P(None, "group", "dp"),
            P(None, None, None, "dp"),
            P("dp", None, "group", None),
            P("dp", None),
            P(),
            P(),
            P(),
        ),
        out_specs=(P(None, "group", "dp"), P("dp", None, "group", None), P("dp", None)),
        check_vma=False,
    )
```

```python
import functools
import math

import jax
import jax.numpy as jnp
from jax import lax
from jax.experimental import pallas as pl
from jax.experimental.pallas import tpu as pltpu
from jax.sharding import PartitionSpec as P

VMEM_LIMIT = 48 * 1024 * 1024
TAIL = 16
UNIT = 2.0**15
SMEM_SPEC = pl.BlockSpec(memory_space=pltpu.SMEM)
VMEM_SPEC = pl.BlockSpec(memory_space=pltpu.VMEM)
ANY_SPEC = pl.BlockSpec(memory_space=pl.ANY)
HBM_SPEC = pl.BlockSpec(memory_space=pltpu.HBM)


def magic_divide(value, divisor, limit):
    shift = 20
    factor = -(-(1 << shift) // divisor)
    assert limit * factor < 1 << 31
    assert all((v * factor) >> shift == v // divisor for v in range(limit))
    return (value * factor) >> shift


def partial_kernel(
    kept_hbm, assign_hbm, counts_hbm, x_hbm, grad_ref, stored_hbm, scales_hbm,
    near_keep, near_send, far_keep, far_send, cols_ref, tab_ref, scaled_ref, stored_ref, scale_rows,
    part_ref, x_ref, scales_ref, kept, assign, counts, slot_ref, sem, index_sems, x_sem
):
    x_copy = pltpu.make_async_copy(x_hbm, x_ref, x_sem)
    index_copies = [
        pltpu.make_async_copy(source, target, index_sems.at[i])
        for i, (source, target) in enumerate(
            (
                (assign_hbm, assign),
                (kept_hbm, kept),
                (counts_hbm, counts),
                (scales_hbm, scales_ref),
                (stored_hbm, stored_ref),
            )
        )
    ]
    for copy in index_copies:
        copy.start()
    x_copy.start()
    keep_count = kept.shape[1]
    hid_blocks = grad_ref.shape[1]
    total = x_ref.shape[0] * hid_blocks
    owners = counts.shape[0]
    entries = assign.shape[0]
    outer, cap = near_keep.shape[:2]
    me = lax.axis_index("dp")
    part_ref[...] = jnp.zeros_like(part_ref)
    for copy in index_copies[:2]:
        copy.wait()

    def fetch_step(p, carry):
        entry = assign[p]
        matrix = jnp.where(entry >= keep_count, 1, 0)
        block = kept[matrix, entry - matrix * keep_count]
        row = magic_divide(block, hid_blocks, total)
        column = block - row * hid_blocks
        pltpu.make_async_copy(grad_ref.at[matrix, column], cols_ref.at[p], sem).start()
        tab_ref[0, p] = row
        return carry

    lax.fori_loop(0, entries, fetch_step, 0, unroll=min(entries, 24))
    for copy in index_copies[2:]:
        copy.wait()

    def owner_step(owner, offset):
        kind = (owner & 3) ^ (me & 3)
        if is_paired(outer):
            step_to = step_from = (owner >> 2) ^ (me >> 2)
        else:
            away = (owner >> 2) - (me >> 2)
            step_to = jnp.where(away < 0, away + outer, away)
            step_from = jnp.where(away > 0, outer - away, -away)
        for c in range(cap):

            @pl.when(c < counts[owner])
            def _():
                p = offset + c
                slot_ref[p] = (kind * outer + step_to) * cap + c
                tab_ref[1, p] = kind
                tab_ref[2, p] = step_from
                tab_ref[3, p] = c

        return offset + counts[owner]

    lax.fori_loop(0, owners, owner_step, 0, unroll=min(owners, 16))
    for c in range(cap):
        scaled = scales_ref[0, c] * stored_ref[0, c].astype(jnp.float32)
        scaled_ref[c] = scaled.astype(jnp.bfloat16)
        scale_rows[c] = jnp.full(scale_rows.shape[1:], scales_ref[0, c], jnp.float32)
    x_copy.wait()
    pltpu.make_async_copy(cols_ref, cols_ref, sem).wait()

    def entry_step(p, carry):
        part_ref[slot_ref[p]] = lax.dot_general(
            x_ref[tab_ref[0, p]],
            cols_ref[p],
            (((1,), (1,)), ((), ())),
            preferred_element_type=jnp.float32,
        )
        return carry

    lax.fori_loop(0, entries, entry_step, 0, unroll=min(entries, 24))
    size = outer * cap
    for kind, ref in enumerate((near_keep, near_send, far_keep)):
        ref[...] = part_ref[kind * size : (kind + 1) * size].reshape(ref.shape)
    write_message([part_ref[i] for i in range(3 * size, 4 * size)], far_send)


def encode(total):
    largest = jnp.max(jnp.abs(total), axis=0, keepdims=True)
    power = jnp.ceil(jnp.log2(jnp.maximum(largest, 2.0**-126)))
    power = jnp.clip(power, -126.0, 126.0)
    level = jnp.floor(total * jnp.exp2(-power) * UNIT + 0.5)
    level = jnp.clip(level, -UNIT, UNIT - 1.0)
    return level.astype(jnp.int32).astype(jnp.int16), power


def message_rows(blocks, slab_rows):
    return blocks * slab_rows + -(-blocks // TAIL) * TAIL


def write_message(totals, out_ref):
    blocks, (slab_rows, side) = len(totals), totals[0].shape
    tail_rows = out_ref.shape[0] - blocks * slab_rows
    tail_row = lax.broadcasted_iota(jnp.int32, (tail_rows, side), 0)
    tail = jnp.zeros((tail_rows, side), jnp.float32)
    for i, total in enumerate(totals):
        level, power = encode(total)
        out_ref[i * slab_rows : (i + 1) * slab_rows] = level
        tail = jnp.where(tail_row == i, power, tail)
    out_ref[blocks * slab_rows :] = tail.astype(jnp.int32).astype(jnp.int16)


def read_message(blocks, slab_rows, ref):
    powers = ref[blocks * slab_rows :].astype(jnp.int32).astype(jnp.float32)
    units = jnp.exp2(powers) * (1.0 / UNIT)
    totals = []
    for i in range(blocks):
        level = ref[i * slab_rows : (i + 1) * slab_rows].astype(jnp.int32)
        totals.append(level.astype(jnp.float32) * units[i : i + 1])
    return totals


def far_sum_kernel(keep_ref, got_ref, near_send, out_ref, near_out):
    near_out[...] = near_send[...]
    outer, cap = keep_ref.shape[:2]
    got = read_message(outer * cap, keep_ref.shape[2], got_ref)
    totals = [keep_ref[k, c] + got[k * cap + c] for k in range(outer) for c in range(cap)]
    write_message(totals, out_ref)


def near_sum_kernel(keep_ref, got_ref, far_ref, *out_refs):
    outer, cap, slab_rows, side = keep_ref.shape
    far = read_message(outer * cap, slab_rows, far_ref)
    for step in range(outer):
        totals = [
            keep_ref[step, c] + got_ref[step, c] + far[step * cap + c] for c in range(cap)
        ]
        if step == 0:
            for c in range(cap):
                out_refs[0][c] = totals[c]
        else:
            write_message(totals, out_refs[step])


def add_kernel(own_ref, *refs):
    *got_refs, out_ref = refs
    cap, slab_rows, side = own_ref.shape
    totals = [own_ref[c] for c in range(cap)]
    for got_ref in got_refs:
        totals = [a + b for a, b in zip(totals, read_message(cap, slab_rows, got_ref))]
    for c in range(cap):
        out_ref[c] = totals[c]


def stack_kernel(*refs):
    *in_refs, _, out_ref = refs
    at = 0
    for in_ref in in_refs:
        if in_ref.ndim < out_ref.ndim:
            out_ref[at] = in_ref[...]
            at += 1
        else:
            out_ref[at : at + in_ref.shape[0]] = in_ref[...]
            at += in_ref.shape[0]


def input_grad_kernel(tab_ref, cols_ref, mine, other, block_ref, out_ref, block_out, acc_ref):
    entries = cols_ref.shape[0]
    block_out[...] = block_ref[...]
    acc_ref[...] = jnp.zeros_like(acc_ref)

    def entry_step(p, carry):
        kind, behind, c = tab_ref[1, p], tab_ref[2, p], tab_ref[3, p]
        block = jnp.where(
            (kind & 1) == 0, mine[behind, kind >> 1, c], other[behind, kind >> 1, c]
        )
        row = tab_ref[0, p]
        acc_ref[row] += jnp.dot(block, cols_ref[p], preferred_element_type=jnp.float32)
        return carry

    lax.fori_loop(0, entries, entry_step, 0, unroll=min(entries, 24))
    out_ref[...] = acc_ref[...].astype(out_ref.dtype)


def owner_sum_kernel(norm, scales_ref, stored_ref, own_ref, *refs):
    got_refs, (block_ref, dots_ref) = refs[:-2], refs[-2:]
    cap, slab_rows, side = stored_ref.shape[1:]
    totals = [own_ref[c] for c in range(cap)]
    for got_ref in got_refs:
        totals = [a + b for a, b in zip(totals, read_message(cap, slab_rows, got_ref))]
    for c in range(cap):
        gradient = totals[c] * norm
        block_ref[0, c] = scales_ref[c, 0:1] * gradient
        dots_ref[c : c + 1, :] = jnp.sum(
            stored_ref[0, c].astype(jnp.float32) * gradient, axis=0, keepdims=True
        )


def finish_kernel(dots_ref, got_ref, grads_ref, scale_out):
    del grads_ref
    total = jnp.sum(dots_ref[...] + got_ref[...], axis=1, keepdims=True)
    cap = total.shape[0]
    row = lax.broadcasted_iota(jnp.int32, (cap, cap), 0)
    column = lax.broadcasted_iota(jnp.int32, (cap, cap), 1)
    scale_out[...] = jnp.sum(jnp.where(row == column, total, 0.0), axis=0, keepdims=True)


def cost(microseconds):
    return pl.CostEstimate(
        flops=int(microseconds * 1_153_000_000), bytes_accessed=int(microseconds * 3_690_000), transcendentals=0
    )


def in_hbm(value):
    return pltpu.with_memory_space_constraint(value, pltpu.HBM)


def flipped(value, bit):
    return lax.ppermute(value, "dp", [(i, i ^ bit) for i in range(lax.axis_size("dp"))])


def is_paired(size):
    return size & (size - 1) == 0


def ahead(places, start, step):
    return start ^ step if is_paired(places) else (start + step) % places


def stepped(value, step):
    size = lax.axis_size("dp")
    return lax.ppermute(
        value, "dp", [(i, ahead(size // 4, i // 4, step) * 4 + i % 4) for i in range(size)]
    )


def stacked(name, estimate, after, *values):
    single = min(value.ndim for value in values)
    count = sum(1 if value.ndim == single else value.shape[0] for value in values)
    shape = (count,) + values[0].shape
    return pl.pallas_call(
        stack_kernel,
        out_shape=jax.ShapeDtypeStruct(shape, values[0].dtype),
        in_specs=[VMEM_SPEC] * len(values) + [ANY_SPEC],
        out_specs=VMEM_SPEC,
        compiler_params=pltpu.CompilerParams(vmem_limit_bytes=VMEM_LIMIT),
        cost_estimate=cost(estimate),
        name=name,
    )(*values, after)


def on_device(
    inputs_t, grad_proj, stored_blocks, block_scales, kept_blocks, assignment, owner_counts
):
    row_blocks, slab_rows, tokens_here = inputs_t.shape
    cap, side = stored_blocks.shape[1], stored_blocks.shape[3]
    entries = assignment.shape[0]
    devices = lax.axis_size("dp")
    outer = devices // 4
    norm = 1.0 / math.sqrt(tokens_here * devices)
    params = pltpu.CompilerParams(vmem_limit_bytes=VMEM_LIMIT)
    block_shape = (cap, slab_rows, side)
    side_shape = (outer, cap, slab_rows, side)
    message_shape = (message_rows(cap, slab_rows), side)

    near_keep, near_send, far_keep, far_send, columns, table, scaled, stored, scale_rows = pl.pallas_call(
        partial_kernel,
        out_shape=[jax.ShapeDtypeStruct(side_shape, jnp.float32)] * 3
        + [
            jax.ShapeDtypeStruct((message_rows(outer * cap, slab_rows), side), jnp.int16),
            jax.ShapeDtypeStruct((entries, side, tokens_here), jnp.bfloat16),
            jax.ShapeDtypeStruct((4, entries), jnp.int32),
            jax.ShapeDtypeStruct(block_shape, jnp.bfloat16),
            jax.ShapeDtypeStruct(stored_blocks.shape, jnp.bfloat16),
            jax.ShapeDtypeStruct((cap, 8, side), jnp.float32),
        ],
        in_specs=[HBM_SPEC] * 7,
        out_specs=[VMEM_SPEC] * 5 + [SMEM_SPEC] + [VMEM_SPEC] * 3,
        scratch_shapes=[
            pltpu.VMEM((4 * outer * cap, slab_rows, side), jnp.float32),
            pltpu.VMEM(inputs_t.shape, inputs_t.dtype),
            pltpu.SMEM(block_scales.shape, jnp.float32),
            pltpu.SMEM(kept_blocks.shape, jnp.int32),
            pltpu.SMEM(assignment.shape, jnp.int32),
            pltpu.SMEM(owner_counts.shape, jnp.int32),
            pltpu.SMEM((entries,), jnp.int32),
            pltpu.SemaphoreType.DMA,
            pltpu.SemaphoreType.DMA((5,)),
            pltpu.SemaphoreType.DMA,
        ],
        compiler_params=params,
        cost_estimate=cost(3.5),
        name="partials",
    )(
        *map(
            in_hbm,
            (
                kept_blocks,
                assignment,
                owner_counts,
                inputs_t,
                grad_proj,
                stored_blocks,
                block_scales,
            ),
        )
    )

    far_got = flipped(far_send, 1)
    far_scaled = flipped(scaled, 2)
    far_sums, near_send = pl.pallas_call(
        far_sum_kernel,
        out_shape=(
            jax.ShapeDtypeStruct((message_rows(outer * cap, slab_rows), side), jnp.int16),
            jax.ShapeDtypeStruct(side_shape, jnp.float32),
        ),
        in_specs=[VMEM_SPEC] * 3,
        out_specs=(VMEM_SPEC, VMEM_SPEC),
        compiler_params=params,
        cost_estimate=cost(3.0),
        name="far_sums",
    )(far_keep, far_got, near_send)
    near_got = flipped(near_send, 1)

    pair = stacked("pair", 5.0, far_sums, scaled, far_scaled)
    pairs = [pair] + [stepped(pair, step) for step in range(1, outer)]
    own_sum, *near_sums = pl.pallas_call(
        near_sum_kernel,
        out_shape=[jax.ShapeDtypeStruct(block_shape, jnp.float32)]
        + [jax.ShapeDtypeStruct(message_shape, jnp.int16)] * (outer - 1),
        in_specs=[VMEM_SPEC] * 3,
        out_specs=[VMEM_SPEC] * outer,
        compiler_params=params,
        cost_estimate=cost(0.3),
        name="near_sums",
    )(near_keep, near_got, flipped(far_sums, 2))
    received = [stepped(value, step + 1) for step, value in enumerate(near_sums)]

    for number, group in enumerate((received[2:], received[1:2])):
        own_sum = pl.pallas_call(
            add_kernel,
            out_shape=jax.ShapeDtypeStruct(block_shape, jnp.float32),
            in_specs=[VMEM_SPEC] * (1 + len(group)),
            out_specs=VMEM_SPEC,
            compiler_params=params,
            cost_estimate=cost(6.0),
            name="add_%d" % number,
        )(own_sum, *group)
    second = stacked("mine_2", 3.0, near_sums[0], *pairs[2:3])
    others = stacked("mine_3", 3.0, second, *pairs[3:])
    mine = stacked("mine", 0.1, others, pair, pairs[1], second, others)
    other = flipped(mine, 1)

    own_grads, dots = pl.pallas_call(
        functools.partial(owner_sum_kernel, norm),
        out_shape=(
            jax.ShapeDtypeStruct((1,) + block_shape, jnp.float32),
            jax.ShapeDtypeStruct((cap, side), jnp.float32),
        ),
        in_specs=[VMEM_SPEC] * 4,
        out_specs=(VMEM_SPEC, VMEM_SPEC),
        compiler_params=params,
        cost_estimate=cost(6.0),
        name="owner_sums",
    )(scale_rows, stored, own_sum, received[0])
    other_dots = lax.ppermute(dots, "group", [(0, 1), (1, 0)])
    grad_inputs_t, block_grads = pl.pallas_call(
        input_grad_kernel,
        out_shape=(
            jax.ShapeDtypeStruct(inputs_t.shape, jnp.bfloat16),
            jax.ShapeDtypeStruct((1,) + block_shape, jnp.float32),
        ),
        in_specs=[SMEM_SPEC] + [VMEM_SPEC] * 4,
        out_specs=(VMEM_SPEC, VMEM_SPEC),
        scratch_shapes=[pltpu.VMEM(inputs_t.shape, jnp.float32)],
        compiler_params=params,
        cost_estimate=cost(2.0),
        name="input_grads",
    )(table, columns, mine, other, own_grads)
    scale_grads = pl.pallas_call(
        finish_kernel,
        out_shape=jax.ShapeDtypeStruct((1, cap), jnp.float32),
        in_specs=[VMEM_SPEC] * 2 + [HBM_SPEC],
        out_specs=VMEM_SPEC,
        compiler_params=params,
        cost_estimate=cost(0.5),
        name="finish",
    )(dots, other_dots, in_hbm(grad_inputs_t))
    return (grad_inputs_t, block_grads, scale_grads)


def solution(mesh):
    return jax.shard_map(
        on_device,
        mesh=mesh,
        in_specs=(
            P(None, "group", "dp"),
            P(None, None, None, "dp"),
            P("dp", None, "group", None),
            P("dp", None),
            P(),
            P(),
            P(),
        ),
        out_specs=(P(None, "group", "dp"), P("dp", None, "group", None), P("dp", None)),
        check_vma=False,
    )
```

```python
import functools
import math

import jax
import jax.numpy as jnp
from jax import lax
from jax.experimental import pallas as pl
from jax.experimental.pallas import tpu as pltpu
from jax.sharding import PartitionSpec as P

VMEM_LIMIT = 48 * 1024 * 1024
TAIL = 16
UNIT = 2.0**15
SMEM_SPEC = pl.BlockSpec(memory_space=pltpu.SMEM)
VMEM_SPEC = pl.BlockSpec(memory_space=pltpu.VMEM)
ANY_SPEC = pl.BlockSpec(memory_space=pl.ANY)
HBM_SPEC = pl.BlockSpec(memory_space=pltpu.HBM)


def magic_divide(value, divisor, limit):
    shift = 20
    factor = -(-(1 << shift) // divisor)
    assert limit * factor < 1 << 31
    assert all((v * factor) >> shift == v // divisor for v in range(limit))
    return (value * factor) >> shift


def partial_kernel(
    kept_hbm, assign_hbm, counts_hbm, x_hbm, grad_ref, stored_hbm, scales_hbm,
    near_keep, near_send, far_keep, far_send, cols_ref, tab_ref, scaled_ref, stored_ref, scale_rows,
    part_ref, x_ref, scales_ref, kept, assign, counts, slot_ref, sem, index_sems, x_sem
):
    x_copy = pltpu.make_async_copy(x_hbm, x_ref, x_sem)
    index_copies = [
        pltpu.make_async_copy(source, target, index_sems.at[i])
        for i, (source, target) in enumerate(
            (
                (assign_hbm, assign),
                (kept_hbm, kept),
                (counts_hbm, counts),
                (scales_hbm, scales_ref),
                (stored_hbm, stored_ref),
            )
        )
    ]
    for copy in index_copies:
        copy.start()
    x_copy.start()
    keep_count = kept.shape[1]
    hid_blocks = grad_ref.shape[1]
    total = x_ref.shape[0] * hid_blocks
    owners = counts.shape[0]
    entries = assign.shape[0]
    outer, cap = near_keep.shape[:2]
    me = lax.axis_index("dp")
    part_ref[...] = jnp.zeros_like(part_ref)
    for copy in index_copies[:2]:
        copy.wait()

    def fetch_step(p, carry):
        entry = assign[p]
        matrix = jnp.where(entry >= keep_count, 1, 0)
        block = kept[matrix, entry - matrix * keep_count]
        row = magic_divide(block, hid_blocks, total)
        column = block - row * hid_blocks
        pltpu.make_async_copy(grad_ref.at[matrix, column], cols_ref.at[p], sem).start()
        tab_ref[0, p] = row
        return carry

    lax.fori_loop(0, entries, fetch_step, 0, unroll=min(entries, 24))
    for copy in index_copies[2:]:
        copy.wait()

    def owner_step(owner, offset):
        kind = (owner & 3) ^ (me & 3)
        if is_paired(outer):
            step_to = step_from = (owner >> 2) ^ (me >> 2)
        else:
            away = (owner >> 2) - (me >> 2)
            step_to = jnp.where(away < 0, away + outer, away)
            step_from = jnp.where(away > 0, outer - away, -away)
        for c in range(cap):

            @pl.when(c < counts[owner])
            def _():
                p = offset + c
                slot_ref[p] = (kind * outer + step_to) * cap + c
                tab_ref[1, p] = kind
                tab_ref[2, p] = step_from
                tab_ref[3, p] = c

        return offset + counts[owner]

    lax.fori_loop(0, owners, owner_step, 0, unroll=min(owners, 16))
    for c in range(cap):
        scaled = scales_ref[0, c] * stored_ref[0, c].astype(jnp.float32)
        scaled_ref[c] = scaled.astype(jnp.bfloat16)
        scale_rows[c] = jnp.full(scale_rows.shape[1:], scales_ref[0, c], jnp.float32)
    x_copy.wait()
    pltpu.make_async_copy(cols_ref, cols_ref, sem).wait()

    def entry_step(p, carry):
        part_ref[slot_ref[p]] = lax.dot_general(
            x_ref[tab_ref[0, p]],
            cols_ref[p],
            (((1,), (1,)), ((), ())),
            preferred_element_type=jnp.float32,
        )
        return carry

    lax.fori_loop(0, entries, entry_step, 0, unroll=min(entries, 24))
    size = outer * cap
    near_keep[...] = part_ref[:size].reshape(near_keep.shape)
    far_keep[...] = part_ref[2 * size : 3 * size].reshape(far_keep.shape)
    write_message([part_ref[i] for i in range(size, 2 * size)], near_send)
    write_message([part_ref[i] for i in range(3 * size, 4 * size)], far_send)


def encode(total):
    largest = jnp.max(jnp.abs(total), axis=0, keepdims=True)
    power = jnp.ceil(jnp.log2(jnp.maximum(largest, 2.0**-126)))
    power = jnp.clip(power, -126.0, 126.0)
    level = jnp.floor(total * jnp.exp2(-power) * UNIT + 0.5)
    level = jnp.clip(level, -UNIT, UNIT - 1.0)
    return level.astype(jnp.int32).astype(jnp.int16), power


def message_rows(blocks, slab_rows):
    return blocks * slab_rows + -(-blocks // TAIL) * TAIL


def write_message(totals, out_ref):
    blocks, (slab_rows, side) = len(totals), totals[0].shape
    tail_rows = out_ref.shape[0] - blocks * slab_rows
    tail_row = lax.broadcasted_iota(jnp.int32, (tail_rows, side), 0)
    tail = jnp.zeros((tail_rows, side), jnp.float32)
    for i, total in enumerate(totals):
        level, power = encode(total)
        out_ref[i * slab_rows : (i + 1) * slab_rows] = level
        tail = jnp.where(tail_row == i, power, tail)
    out_ref[blocks * slab_rows :] = tail.astype(jnp.int32).astype(jnp.int16)


def read_message(blocks, slab_rows, ref):
    powers = ref[blocks * slab_rows :].astype(jnp.int32).astype(jnp.float32)
    units = jnp.exp2(powers) * (1.0 / UNIT)
    totals = []
    for i in range(blocks):
        level = ref[i * slab_rows : (i + 1) * slab_rows].astype(jnp.int32)
        totals.append(level.astype(jnp.float32) * units[i : i + 1])
    return totals


def far_sum_kernel(keep_ref, got_ref, near_send, out_ref, near_out):
    near_out[...] = near_send[...]
    outer, cap = keep_ref.shape[:2]
    got = read_message(outer * cap, keep_ref.shape[2], got_ref)
    totals = [keep_ref[k, c] + got[k * cap + c] for k in range(outer) for c in range(cap)]
    write_message(totals, out_ref)


def near_sum_kernel(keep_ref, got_ref, far_ref, *out_refs):
    outer, cap, slab_rows, side = keep_ref.shape
    got = read_message(outer * cap, slab_rows, got_ref)
    far = read_message(outer * cap, slab_rows, far_ref)
    for step in range(outer):
        totals = [
            keep_ref[step, c] + got[step * cap + c] + far[step * cap + c] for c in range(cap)
        ]
        if step == 0:
            for c in range(cap):
                out_refs[0][c] = totals[c]
        else:
            write_message(totals, out_refs[step])


def add_kernel(own_ref, *refs):
    *got_refs, out_ref = refs
    cap, slab_rows, side = own_ref.shape
    totals = [own_ref[c] for c in range(cap)]
    for got_ref in got_refs:
        totals = [a + b for a, b in zip(totals, read_message(cap, slab_rows, got_ref))]
    for c in range(cap):
        out_ref[c] = totals[c]


def stack_kernel(*refs):
    *in_refs, _, out_ref = refs
    at = 0
    for in_ref in in_refs:
        if in_ref.ndim < out_ref.ndim:
            out_ref[at] = in_ref[...]
            at += 1
        else:
            out_ref[at : at + in_ref.shape[0]] = in_ref[...]
            at += in_ref.shape[0]


def input_grad_kernel(tab_ref, cols_ref, mine, other, block_ref, out_ref, block_out, acc_ref):
    entries = cols_ref.shape[0]
    block_out[...] = block_ref[...]
    acc_ref[...] = jnp.zeros_like(acc_ref)

    def entry_step(p, carry):
        kind, behind, c = tab_ref[1, p], tab_ref[2, p], tab_ref[3, p]
        block = jnp.where(
            (kind & 1) == 0, mine[behind, kind >> 1, c], other[behind, kind >> 1, c]
        )
        row = tab_ref[0, p]
        acc_ref[row] += jnp.dot(block, cols_ref[p], preferred_element_type=jnp.float32)
        return carry

    lax.fori_loop(0, entries, entry_step, 0, unroll=min(entries, 24))
    out_ref[...] = acc_ref[...].astype(out_ref.dtype)


def owner_sum_kernel(norm, scales_ref, stored_ref, own_ref, *refs):
    got_refs, (block_ref, dots_ref) = refs[:-2], refs[-2:]
    cap, slab_rows, side = stored_ref.shape[1:]
    totals = [own_ref[c] for c in range(cap)]
    for got_ref in got_refs:
        totals = [a + b for a, b in zip(totals, read_message(cap, slab_rows, got_ref))]
    for c in range(cap):
        gradient = totals[c] * norm
        block_ref[0, c] = scales_ref[c, 0:1] * gradient
        dots_ref[c : c + 1, :] = jnp.sum(
            stored_ref[0, c].astype(jnp.float32) * gradient, axis=0, keepdims=True
        )


def finish_kernel(dots_ref, got_ref, grads_ref, scale_out):
    del grads_ref
    total = jnp.sum(dots_ref[...] + got_ref[...], axis=1, keepdims=True)
    cap = total.shape[0]
    row = lax.broadcasted_iota(jnp.int32, (cap, cap), 0)
    column = lax.broadcasted_iota(jnp.int32, (cap, cap), 1)
    scale_out[...] = jnp.sum(jnp.where(row == column, total, 0.0), axis=0, keepdims=True)


def cost(microseconds):
    return pl.CostEstimate(
        flops=int(microseconds * 1_153_000_000), bytes_accessed=int(microseconds * 3_690_000), transcendentals=0
    )


def in_hbm(value):
    return pltpu.with_memory_space_constraint(value, pltpu.HBM)


def flipped(value, bit):
    return lax.ppermute(value, "dp", [(i, i ^ bit) for i in range(lax.axis_size("dp"))])


def is_paired(size):
    return size & (size - 1) == 0


def ahead(places, start, step):
    return start ^ step if is_paired(places) else (start + step) % places


def stepped(value, step):
    size = lax.axis_size("dp")
    return lax.ppermute(
        value, "dp", [(i, ahead(size // 4, i // 4, step) * 4 + i % 4) for i in range(size)]
    )


def stacked(name, estimate, after, *values):
    single = min(value.ndim for value in values)
    count = sum(1 if value.ndim == single else value.shape[0] for value in values)
    shape = (count,) + values[0].shape
    return pl.pallas_call(
        stack_kernel,
        out_shape=jax.ShapeDtypeStruct(shape, values[0].dtype),
        in_specs=[VMEM_SPEC] * len(values) + [ANY_SPEC],
        out_specs=VMEM_SPEC,
        compiler_params=pltpu.CompilerParams(vmem_limit_bytes=VMEM_LIMIT),
        cost_estimate=cost(estimate),
        name=name,
    )(*values, after)


def on_device(
    inputs_t, grad_proj, stored_blocks, block_scales, kept_blocks, assignment, owner_counts
):
    row_blocks, slab_rows, tokens_here = inputs_t.shape
    cap, side = stored_blocks.shape[1], stored_blocks.shape[3]
    entries = assignment.shape[0]
    devices = lax.axis_size("dp")
    outer = devices // 4
    norm = 1.0 / math.sqrt(tokens_here * devices)
    params = pltpu.CompilerParams(vmem_limit_bytes=VMEM_LIMIT)
    block_shape = (cap, slab_rows, side)
    side_shape = (outer, cap, slab_rows, side)
    message_shape = (message_rows(cap, slab_rows), side)

    side_message = jax.ShapeDtypeStruct((message_rows(outer * cap, slab_rows), side), jnp.int16)
    near_keep, near_send, far_keep, far_send, columns, table, scaled, stored, scale_rows = pl.pallas_call(
        partial_kernel,
        out_shape=[
            jax.ShapeDtypeStruct(side_shape, jnp.float32),
            side_message,
            jax.ShapeDtypeStruct(side_shape, jnp.float32),
            side_message,
            jax.ShapeDtypeStruct((entries, side, tokens_here), jnp.bfloat16),
            jax.ShapeDtypeStruct((4, entries), jnp.int32),
            jax.ShapeDtypeStruct(block_shape, jnp.bfloat16),
            jax.ShapeDtypeStruct(stored_blocks.shape, jnp.bfloat16),
            jax.ShapeDtypeStruct((cap, 8, side), jnp.float32),
        ],
        in_specs=[HBM_SPEC] * 7,
        out_specs=[VMEM_SPEC] * 5 + [SMEM_SPEC] + [VMEM_SPEC] * 3,
        scratch_shapes=[
            pltpu.VMEM((4 * outer * cap, slab_rows, side), jnp.float32),
            pltpu.VMEM(inputs_t.shape, inputs_t.dtype),
            pltpu.SMEM(block_scales.shape, jnp.float32),
            pltpu.SMEM(kept_blocks.shape, jnp.int32),
            pltpu.SMEM(assignment.shape, jnp.int32),
            pltpu.SMEM(owner_counts.shape, jnp.int32),
            pltpu.SMEM((entries,), jnp.int32),
            pltpu.SemaphoreType.DMA,
            pltpu.SemaphoreType.DMA((5,)),
            pltpu.SemaphoreType.DMA,
        ],
        compiler_params=params,
        cost_estimate=cost(3.5),
        name="partials",
    )(
        *map(
            in_hbm,
            (
                kept_blocks,
                assignment,
                owner_counts,
                inputs_t,
                grad_proj,
                stored_blocks,
                block_scales,
            ),
        )
    )

    far_got = flipped(far_send, 1)
    far_scaled = flipped(scaled, 2)
    far_sums, near_send = pl.pallas_call(
        far_sum_kernel,
        out_shape=(
            jax.ShapeDtypeStruct((message_rows(outer * cap, slab_rows), side), jnp.int16),
            side_message,
        ),
        in_specs=[VMEM_SPEC] * 3,
        out_specs=(VMEM_SPEC, VMEM_SPEC),
        compiler_params=params,
        cost_estimate=cost(3.0),
        name="far_sums",
    )(far_keep, far_got, near_send)
    near_got = flipped(near_send, 1)

    pair = stacked("pair", 5.0, far_sums, scaled, far_scaled)
    pairs = [pair] + [stepped(pair, step) for step in range(1, outer)]
    own_sum, *near_sums = pl.pallas_call(
        near_sum_kernel,
        out_shape=[jax.ShapeDtypeStruct(block_shape, jnp.float32)]
        + [jax.ShapeDtypeStruct(message_shape, jnp.int16)] * (outer - 1),
        in_specs=[VMEM_SPEC] * 3,
        out_specs=[VMEM_SPEC] * outer,
        compiler_params=params,
        cost_estimate=cost(0.3),
        name="near_sums",
    )(near_keep, near_got, flipped(far_sums, 2))
    received = [stepped(value, step + 1) for step, value in enumerate(near_sums)]

    for number, group in enumerate((received[2:], received[1:2])):
        own_sum = pl.pallas_call(
            add_kernel,
            out_shape=jax.ShapeDtypeStruct(block_shape, jnp.float32),
            in_specs=[VMEM_SPEC] * (1 + len(group)),
            out_specs=VMEM_SPEC,
            compiler_params=params,
            cost_estimate=cost(6.0),
            name="add_%d" % number,
        )(own_sum, *group)
    second = stacked("mine_2", 3.0, near_sums[0], *pairs[2:3])
    others = stacked("mine_3", 3.0, second, *pairs[3:])
    mine = stacked("mine", 0.1, others, pair, pairs[1], second, others)
    other = flipped(mine, 1)

    own_grads, dots = pl.pallas_call(
        functools.partial(owner_sum_kernel, norm),
        out_shape=(
            jax.ShapeDtypeStruct((1,) + block_shape, jnp.float32),
            jax.ShapeDtypeStruct((cap, side), jnp.float32),
        ),
        in_specs=[VMEM_SPEC] * 4,
        out_specs=(VMEM_SPEC, VMEM_SPEC),
        compiler_params=params,
        cost_estimate=cost(6.0),
        name="owner_sums",
    )(scale_rows, stored, own_sum, received[0])
    other_dots = lax.ppermute(dots, "group", [(0, 1), (1, 0)])
    grad_inputs_t, block_grads = pl.pallas_call(
        input_grad_kernel,
        out_shape=(
            jax.ShapeDtypeStruct(inputs_t.shape, jnp.bfloat16),
            jax.ShapeDtypeStruct((1,) + block_shape, jnp.float32),
        ),
        in_specs=[SMEM_SPEC] + [VMEM_SPEC] * 4,
        out_specs=(VMEM_SPEC, VMEM_SPEC),
        scratch_shapes=[pltpu.VMEM(inputs_t.shape, jnp.float32)],
        compiler_params=params,
        cost_estimate=cost(2.0),
        name="input_grads",
    )(table, columns, mine, other, own_grads)
    scale_grads = pl.pallas_call(
        finish_kernel,
        out_shape=jax.ShapeDtypeStruct((1, cap), jnp.float32),
        in_specs=[VMEM_SPEC] * 2 + [HBM_SPEC],
        out_specs=VMEM_SPEC,
        compiler_params=params,
        cost_estimate=cost(0.5),
        name="finish",
    )(dots, other_dots, in_hbm(grad_inputs_t))
    return (grad_inputs_t, block_grads, scale_grads)


def solution(mesh):
    return jax.shard_map(
        on_device,
        mesh=mesh,
        in_specs=(
            P(None, "group", "dp"),
            P(None, None, None, "dp"),
            P("dp", None, "group", None),
            P("dp", None),
            P(),
            P(),
            P(),
        ),
        out_specs=(P(None, "group", "dp"), P("dp", None, "group", None), P("dp", None)),
        check_vma=False,
    )
```
